512 devices in a mesh: dp: 16 (over y, x), expert: 32 (over z, core).
Axes of the slice: x: 4, y: 4, z: 16, core: 2. Of those that a mesh axis runs over, the one named last changes fastest.
Arguments:
- tokens: bfloat16 [65536, 2560], P(('dp', 'expert')), may hold values from -6 to 6
- out_grad: bfloat16 [65536, 2560], P(('dp', 'expert')), may hold values from -0.59765625 to 0.59765625
- expert_ids: int32 [65536, 2], P(('dp', 'expert')), may hold values from 0 to 31, all different within a row; in each aligned block of 128 rows (0 to 127, 128 to 255, ...) at most 9 rows name the same one
- gate_values: float32 [65536, 2], P(('dp', 'expert')), may hold values from 0.05 to 0.5
- frozen_gate: bfloat16 [32, 2560, 768], P('expert', 'dp'), may hold values from -0.125 to 0.125
- frozen_up: bfloat16 [32, 2560, 768], P('expert', 'dp'), may hold values from -0.125 to 0.125
- locked_down_weight: bfloat16 [32, 2560, 768], P('expert', 'dp'), may hold values from -0.21875 to 0.21875
- gate_adapter_first: bfloat16 [32, 2560, 16], P('expert'), may hold values from -0.125 to 0.125
- gate_adapter_second: bfloat16 [32, 16, 768], P('expert'), may hold values from -1.5 to 1.5
- up_adapter_first: bfloat16 [32, 2560, 16], P('expert'), may hold values from -0.125 to 0.125
- up_adapter_second: bfloat16 [32, 16, 768], P('expert'), may hold values from -1.5 to 1.5
- down_adapter_first: bfloat16 [32, 768, 16], P('expert'), may hold values from -0.21875 to 0.21875
- down_adapter_second: bfloat16 [32, 16, 2560], P('expert'), may hold values from -1.5 to 1.5
Outputs:
- token_grad: bfloat16 [65536, 2560], P(('dp', 'expert'))
- gate_grad: float32 [65536, 2], P(('dp', 'expert'))
- grad_gate_in: float32 [32, 2560, 16], P('expert')
- grad_gate_out: float32 [32, 16, 768], P('expert')
- grad_up_in: float32 [32, 2560, 16], P('expert')
- grad_up_out: float32 [32, 16, 768], P('expert')
- grad_down_in: float32 [32, 768, 16], P('expert')
- grad_down_out: float32 [32, 16, 2560], P('expert')
The draws below stay inside these ranges and needn't reach their ends.
Inputs may be any that keep to these rules, and one draw needn't show every extreme that they name: `expert_ids`: each token names 2 different experts. In the rows of one device no expert is named by more than 9 rows, a bound that some block reaches of one device.
All inputs are finite; a program needn't handle non-finite values.
Results may differ from the reference program's by a relative error of at most 0.025.
Values may be sent and summed in bfloat16 or wider, within the bound.
A program may use at most 128 MiB of HBM per device.

```python
import math
import jax
import jax.numpy as jnp
import numpy as np
from jax import lax

D = 2560
FF = 768
RANK = 16
TOP = 2
TOK_DEV = 128
EXPERTS = 32
CAP = 9
TOKENS = 65536


def level_of(rng, extent, shards, least, largest):
    def one(axis_at, parts):
        draws = jax.random.uniform(jax.random.fold_in(jax.random.fold_in(rng, 6), axis_at), (parts,), jnp.float32, least / len(shards), largest / len(shards))
        return jnp.repeat(jnp.exp(draws), extent[axis_at] // parts).reshape((-1,) + (1,) * (len(extent) - axis_at - 1))

    loudness = one(*shards[0])
    for cut in shards[1:]:
        loudness = loudness * one(*cut)
    return loudness


def assign_block(stream_key, own, number, rows, amount, top, most, lean):
    sequence = jax.random.permutation(stream_key, amount)
    crowded, usual = portions_of(amount, rows * top, most, lean, True), portions_of(amount, rows * top, most, lean, False)
    places = jnp.arange(amount)

    def named(tallies, offset_by):
        used = int((tallies > 0).sum())
        fixed = max(1, used // 4)
        shifted = fixed + (places - fixed + offset_by * (used - fixed)) % max(1, amount - fixed)
        return jnp.zeros((amount,), jnp.int32).at[sequence[jnp.where(places < fixed, places, shifted)]].set(jnp.asarray(tallies, jnp.int32))

    tallies = jnp.where(number % 4 == 0, named(crowded, number // 4), named(usual, number - number // 4 - 1))
    mixed = jax.random.permutation(jax.random.fold_in(own, 3), amount)
    giver, taker = mixed[0:amount // 2 * 2:2], mixed[1:amount // 2 * 2:2]
    slack = jnp.minimum(tallies[giver] - 1, most - tallies[taker]) // 2
    slack = jnp.where((giver == sequence[0]) | (taker == sequence[0]) | (tallies[taker] == 0), 0, jnp.maximum(slack, 0))
    shifted = jax.random.randint(jax.random.fold_in(own, 4), (amount // 2,), 0, 1 << 20) % (slack + 1)
    tallies = tallies.at[giver].add(-shifted).at[taker].add(shifted)
    members = jnp.searchsorted(jnp.cumsum(tallies), jnp.arange(rows * top), side="right").astype(jnp.int32)
    table = members.reshape(top, rows).T
    table = table[jax.random.permutation(jax.random.fold_in(own, 1), rows)]
    offset_by = jax.random.randint(jax.random.fold_in(own, 2), (rows, 1), 0, top)
    return jnp.take_along_axis(table, (jnp.arange(top)[None, :] + offset_by) % top, axis=1)


def portions_of(amount, total, limit, slope, full):
    loads = [(1 << 20) // math.isqrt(standing ** slope) + 1 for standing in range(1, amount + 1)]
    largest = limit if full else min(limit, max(-(-total // amount), total * loads[0] // sum(loads)))
    least = 1 if total - largest >= amount - 1 else 0
    holding, spare = [largest] + [least] * (amount - 1), total - largest - least * (amount - 1)
    while spare > 0:
        candidates = [i for i in range(1, amount) if holding[i] < largest] or [i for i in range(1, amount) if holding[i] < limit]
        whole, left = sum([loads[i] for i in candidates]), spare
        for i in candidates:
            extra = min(limit - holding[i], max(1, left * loads[i] // whole), spare)
            holding[i] = holding[i] + extra
            spare = spare - extra
    return np.array(holding)


def bell_draw(key, shape, spread, bound, cuts=(), kind=jnp.bfloat16):
    result = spread * jax.random.normal(key, shape, jnp.float32)
    if cuts:
        result = result * level_of(key, shape, cuts, -0.22, 0.18)
    return jnp.clip(result, -bound, bound).astype(kind)


def setup_inputs(seed: int = 0) -> dict:
    key_list = jax.random.split(jax.random.key(seed), 14)
    tokens = bell_draw(key_list[0], (TOKENS, D), 1.0, 6.0, ((0, 512),))
    out_grad = bell_draw(key_list[1], (TOKENS, D), 0.1, 0.59765625, ((0, 512),))
    expert_ids_keys = jax.random.split(jax.random.fold_in(key_list[2], 1), TOKENS // TOK_DEV)
    expert_ids_turns = jax.random.permutation(jax.random.fold_in(key_list[2], 3), TOKENS // TOK_DEV)
    expert_ids = jax.vmap(lambda own, number: assign_block(jax.random.fold_in(key_list[2], 2), own, number, TOK_DEV, EXPERTS, TOP, CAP, 2))(expert_ids_keys, expert_ids_turns).reshape((TOKENS, TOP))
    gate_values = jnp.clip(0.05 + 0.45 * jax.random.uniform(key_list[3], (TOKENS, TOP), jnp.float32) ** level_of(key_list[3], (TOKENS, TOP), ((0, 512),), -0.2, 0.2), 0.05, 0.5)
    frozen_gate = bell_draw(key_list[4], (EXPERTS, D, FF), D ** -0.5, 0.125, ((0, 32), (1, 16)))
    frozen_up = bell_draw(key_list[5], (EXPERTS, D, FF), D ** -0.5, 0.125, ((0, 32), (1, 16)))
    locked_down_weight = bell_draw(key_list[6], (EXPERTS, D, FF), FF ** -0.5, 0.21875, ((0, 32), (1, 16)))
    gate_adapter_first = bell_draw(key_list[7], (EXPERTS, D, RANK), D ** -0.5, 0.125, ((0, 32),))
    gate_adapter_second = bell_draw(key_list[8], (EXPERTS, RANK, FF), RANK ** -0.5, 1.5, ((0, 32),))
    up_adapter_first = bell_draw(key_list[9], (EXPERTS, D, RANK), D ** -0.5, 0.125, ((0, 32),))
    up_adapter_second = bell_draw(key_list[10], (EXPERTS, RANK, FF), RANK ** -0.5, 1.5, ((0, 32),))
    down_adapter_first = bell_draw(key_list[11], (EXPERTS, FF, RANK), FF ** -0.5, 0.21875, ((0, 32),))
    down_adapter_second = bell_draw(key_list[12], (EXPERTS, RANK, D), RANK ** -0.5, 1.5, ((0, 32),))
    return dict(tokens=tokens, out_grad=out_grad, expert_ids=expert_ids, gate_values=gate_values, frozen_gate=frozen_gate, frozen_up=frozen_up, locked_down_weight=locked_down_weight, gate_adapter_first=gate_adapter_first, gate_adapter_second=gate_adapter_second, up_adapter_first=up_adapter_first, up_adapter_second=up_adapter_second, down_adapter_first=down_adapter_first, down_adapter_second=down_adapter_second)


adapter_scale = 2.0


def matrix_product(left, right):
    return jnp.dot(left, right, preferred_element_type=jnp.float32)


def right_operand_flipped(left, right):
    return lax.dot_general(left, right, (((1,), (1,)), ((), ())), preferred_element_type=jnp.float32)


def left_operand_flipped(left, right):
    return lax.dot_general(left, right, (((0,), (0,)), ((), ())), preferred_element_type=jnp.float32)


def expert_adapter_rows(row_inputs, row_gradient, row_weighting, locked_gate_weight, locked_up_weight, gate_weight_matrix, up_weight_matrix, down_weight_matrix, gate_first_factor, gate_second_factor, up_first_factor, up_second_factor, down_first_factor, down_second_factor):
    gate_reduced_rows = matrix_product(row_inputs, gate_first_factor).astype(jnp.bfloat16)
    up_reduced_rows = matrix_product(row_inputs, up_first_factor).astype(jnp.bfloat16)
    gate_before_activation = locked_gate_weight + adapter_scale * matrix_product(gate_reduced_rows, gate_second_factor)
    up_before_activation = locked_up_weight + adapter_scale * matrix_product(up_reduced_rows, up_second_factor)
    sigmoid_gate = jax.nn.sigmoid(gate_before_activation)
    activation = gate_before_activation * sigmoid_gate
    hidden_rows = (activation * up_before_activation).astype(jnp.bfloat16)
    hidden_reduced_rows = matrix_product(hidden_rows, down_first_factor).astype(jnp.bfloat16)
    expert_result = right_operand_flipped(hidden_rows, down_weight_matrix) + adapter_scale * matrix_product(hidden_reduced_rows, down_second_factor)
    grad_wide = row_gradient.astype(jnp.float32)
    slot_gate_values = jnp.sum(expert_result * grad_wide, axis=1)
    incoming_gradient = (row_weighting[:, None] * grad_wide).astype(jnp.bfloat16)
    incoming_reduced_gradient = right_operand_flipped(incoming_gradient, down_second_factor).astype(jnp.bfloat16)
    hidden_gradient = matrix_product(incoming_gradient, down_weight_matrix) + adapter_scale * right_operand_flipped(incoming_reduced_gradient, down_first_factor)
    gate_gradient_before = (hidden_gradient * up_before_activation * sigmoid_gate * (1.0 + gate_before_activation * (1.0 - sigmoid_gate))).astype(jnp.bfloat16)
    up_gradient_before = (hidden_gradient * activation).astype(jnp.bfloat16)
    gate_reduced_gradient = right_operand_flipped(gate_gradient_before, gate_second_factor).astype(jnp.bfloat16)
    up_reduced_gradient = right_operand_flipped(up_gradient_before, up_second_factor).astype(jnp.bfloat16)
    slot_gradient = right_operand_flipped(gate_gradient_before, gate_weight_matrix) + right_operand_flipped(up_gradient_before, up_weight_matrix)
    slot_gradient = slot_gradient + adapter_scale * (right_operand_flipped(gate_reduced_gradient, gate_first_factor) + right_operand_flipped(up_reduced_gradient, up_first_factor))
    slot_gradient = slot_gradient.astype(jnp.bfloat16)
    gradient_tuple = (adapter_scale * left_operand_flipped(row_inputs, gate_reduced_gradient),
             adapter_scale * left_operand_flipped(gate_reduced_rows, gate_gradient_before),
             adapter_scale * left_operand_flipped(row_inputs, up_reduced_gradient),
             adapter_scale * left_operand_flipped(up_reduced_rows, up_gradient_before),
             adapter_scale * left_operand_flipped(hidden_rows, incoming_reduced_gradient),
             adapter_scale * left_operand_flipped(hidden_reduced_rows, incoming_gradient))
    return slot_gradient, slot_gate_values, gradient_tuple


def slot_positions(flat_ids, expert_total):
    onehot = (flat_ids[..., None] == jnp.arange(expert_total, dtype=jnp.int32)).astype(jnp.int32)
    before = jnp.cumsum(onehot, axis=-2) - onehot
    return jnp.sum(before * onehot, axis=-1).astype(jnp.int32)


def reference(tokens, out_grad, expert_ids, gate_values, frozen_gate, frozen_up, locked_down_weight, gate_adapter_first, gate_adapter_second, up_adapter_first, up_adapter_second, down_adapter_first, down_adapter_second):
    blocks = TOKENS // TOK_DEV
    flat_ids = expert_ids.reshape(blocks, TOK_DEV * TOP).astype(jnp.int32)
    slot_index = slot_positions(flat_ids, EXPERTS)
    block_index = jnp.arange(blocks, dtype=jnp.int32)[:, None]
    destination = ((flat_ids * blocks + block_index) * CAP + slot_index).reshape(-1).astype(jnp.int32)
    owners = (jnp.arange(TOKENS * TOP, dtype=jnp.int32) // TOP).astype(jnp.int32)
    table_size = EXPERTS * blocks * CAP
    source = jnp.full((table_size,), TOKENS, jnp.int32).at[destination].set(owners)
    weight_table = jnp.zeros((table_size,), jnp.float32).at[destination].set(gate_values.reshape(-1).astype(jnp.float32))
    tokens_pad = jnp.concatenate([tokens, jnp.zeros((1, D), jnp.bfloat16)], axis=0)
    grads_pad = jnp.concatenate([out_grad, jnp.zeros((1, D), jnp.bfloat16)], axis=0)
    row_count = blocks * CAP

    def per_expert(total, expert_position):
        first = (expert_position * row_count).astype(jnp.int32)
        source_rows = lax.dynamic_slice_in_dim(source, first, row_count)
        row_weighting = lax.dynamic_slice_in_dim(weight_table, first, row_count)
        row_inputs = tokens_pad[source_rows]
        row_gradient = grads_pad[source_rows]
        gate_weight_matrix = frozen_gate[expert_position]
        up_weight_matrix = frozen_up[expert_position]
        locked_gate_weight = matrix_product(row_inputs, gate_weight_matrix)
        locked_up_weight = matrix_product(row_inputs, up_weight_matrix)
        slot_gradient, slot_gate_values, gradient_tuple = expert_adapter_rows(row_inputs, row_gradient, row_weighting, locked_gate_weight, locked_up_weight, gate_weight_matrix, up_weight_matrix, locked_down_weight[expert_position], gate_adapter_first[expert_position], gate_adapter_second[expert_position], up_adapter_first[expert_position], up_adapter_second[expert_position], down_adapter_first[expert_position], down_adapter_second[expert_position])
        total = total.at[source_rows].add(slot_gradient.astype(jnp.float32), mode="drop")
        return total, (slot_gate_values, gradient_tuple)

    start_total = jnp.zeros((TOKENS, D), jnp.float32)
    total, (gate_table, gradient_tuple) = lax.scan(per_expert, start_total, jnp.arange(EXPERTS, dtype=jnp.int32))
    token_grad = total.astype(jnp.bfloat16)
    gate_grad = gate_table.reshape(-1)[destination].reshape(TOKENS, TOP)
    return (token_grad, gate_grad, gradient_tuple[0], gradient_tuple[1], gradient_tuple[2], gradient_tuple[3], gradient_tuple[4], gradient_tuple[5])
```

```python
import functools

import jax
import jax.numpy as jnp
from jax import lax
from jax.experimental import pallas as pl
from jax.experimental.pallas import tpu as pltpu
from jax.sharding import PartitionSpec as P

MESH = pl.DeviceIdType.MESH
bf16 = jnp.bfloat16
f32 = jnp.float32
i32 = jnp.int32

NE, ND = 32, 16
TD, D, F = 128, 2560, 768
H = D // 2
SH = D // ND
ROWS = 288
BW = H + 256
SCALE = 2.0


def nn(a, b):
    return lax.dot_general(a, b, (((1,), (0,)), ((), ())), preferred_element_type=f32)


def nt(a, b):
    return lax.dot_general(a, b, (((1,), (1,)), ((), ())), preferred_element_type=f32)


def tn(a, b):
    return lax.dot_general(a, b, (((0,), (0,)), ((), ())), preferred_element_type=f32)


def iota(shape, axis):
    return lax.broadcasted_iota(i32, shape, axis)


def flag(mask):
    return jnp.where(mask, 1.0, 0.0).astype(bf16)


def loop(n, body):
    def step(k, carry):
        body(k)
        return carry

    lax.fori_loop(0, n, step, 0)


def lanes(n, width=256, start=0):
    return pl.ds(pl.multiple_of(n * width + start, 128), width)


def kernel(
    tok, grd, ids, gates, wg, wu, wd, gfT, gs, ufT, us, dfT, dsec,
    tg_out, gg_out, ggi, ggo, gui, guo, gdi, gdo,
    send, recv, wbuf, sel, perm, permT, fold, unfold, x, g, sg, coef, act, hid, ggp, ugp,
    ad_send, ad_recv, ad_one, ad_all,
    s_send, s_recv, w_send, w_recv, w_own, a_send, a_recv,
):
    me = lax.axis_index("expert")
    dp = lax.axis_index("dp")

    def expert_peer(k):
        z, c = me // 2, me % 2
        m = (k + 1) // 2
        c2 = (c + (k + 1) % 2) % 2
        h = (m + 1) // 2
        dz = h * (m % 2) + (16 - h) * (1 - m % 2)
        return ((z + dz) % 16) * 2 + c2

    def dp_peer(k):
        return (dp + 1 + k) % ND

    bar = pltpu.get_barrier_semaphore()
    loop(NE - 1, lambda k: pl.semaphore_signal(
        bar, inc=1, device_id={"expert": (me + 1 + k) % NE}, device_id_type=MESH))
    loop(ND - 1, lambda k: pl.semaphore_signal(
        bar, inc=1, device_id={"dp": dp_peer(k)}, device_id_type=MESH))

    q512 = iota((512, TD), 0)
    e32 = iota((NE, TD), 0)
    id0, id1 = ids[0:1, :], ids[1:2, :]
    hot = [jnp.where(e32 == id0, 1.0, 0.0), jnp.where(e32 == id1, 1.0, 0.0)]
    earlier = flag(iota((TD, TD), 0) < iota((TD, TD), 1))
    before = nn((hot[0] + hot[1]).astype(bf16), earlier)
    slots = [jnp.sum(before * h, axis=0, keepdims=True).astype(i32) for h in hot]
    keys = [
        jnp.where(slots[0] < 8, id0 * 16 + slots[0], -16),
        jnp.where(slots[1] < 8, id1 * 16 + slots[1], -16),
    ]
    sel[:, 0:TD] = flag((q512 == keys[0]) | (q512 == keys[1]))
    sel[:, TD : 2 * TD] = flag((q512 == keys[0] + 8) | (q512 == keys[1] + 8))
    sel9 = (
        jnp.where(slots[0] == 8, hot[0], 0.0) + jnp.where(slots[1] == 8, hot[1], 0.0)
    ).astype(bf16)
    qa, qb = iota((512, 512), 0), iota((512, 512), 1)
    perm[...] = flag(qb == (qa % 16) * 32 + qa // 16)
    permT[...] = flag(qa == (qb % 16) * 32 + qb // 16)
    cb = qb % 256
    fold[...] = flag(qa == (cb // 8) * 16 + cb % 8 + (qb // 256) * 8)
    ca = qa % 256
    unfold[...] = flag(qb == (ca // 8) * 16 + ca % 8 + (qa // 256) * 8)
    put_weight = flag(iota((512, NE), 0) == iota((512, NE), 1) * 16 + 4)
    take_weight = flag(iota((NE, 512), 1) == iota((NE, 512), 0) * 16 + 4)

    def tail_to_block(buf, nine, extra):
        first = jnp.concatenate([nine[:, j * 128 : (j + 1) * 128] for j in range(16)], axis=0)
        last = jnp.concatenate([nine[:, j * 128 : (j + 1) * 128] for j in range(16, 20)], axis=0)
        send[buf, :, H : H + 128] = nn(perm[...], first).astype(bf16)
        z1 = nn(perm[:, 0:128], last)
        if extra is not None:
            z1 = z1 + nn(put_weight, extra)
        send[buf, :, H + 128 : BW] = z1.astype(bf16)

    def tail_from_block(buf):
        first = nn(permT[...], recv[buf, :, H : H + 128]).astype(bf16)
        last = nn(permT[0:128, :], recv[buf, :, H + 128 : BW]).astype(bf16)
        parts = [first[j * 32 : (j + 1) * 32] for j in range(16)]
        parts += [last[j * 32 : (j + 1) * 32] for j in range(4)]
        return parts

    def dispatch(buf, src, extra):
        def body(n):
            both = jnp.concatenate([src[:, lanes(n)], src[:, lanes(n, start=H)]], axis=0)
            send[buf, :, lanes(n)] = nn(sel[...], both).astype(bf16)

        loop(H // 256, body)
        tail_to_block(buf, nn(sel9, src[...]).astype(bf16), extra)

    def block(p):
        return pl.ds(pl.multiple_of(p * 16, 16), 16)

    def row_copy(buf, there, here):
        return pltpu.make_async_remote_copy(
            src_ref=send.at[buf, block(there)],
            dst_ref=recv.at[buf, block(here)],
            send_sem=s_send.at[buf, there],
            recv_sem=s_recv.at[buf, here],
            device_id={"expert": there},
            device_id_type=MESH,
        )

    def rows_start(buf):
        loop(NE - 1, lambda k: row_copy(buf, expert_peer(k), me).start())
        recv[buf, block(me), :] = send[buf, block(me), :]

    def rows_wait(buf):
        def body(k):
            p = (me + 1 + k) % NE
            row_copy(buf, p, p).wait_recv()

        loop(NE - 1, body)

    def rows_sent(buf):
        def body(k):
            p = (me + 1 + k) % NE
            row_copy(buf, p, p).wait_send()

        loop(NE - 1, body)

    shards = [wg, wu, wd]

    def shard_rows(p):
        return pl.ds(pl.multiple_of(p * SH, 32), SH)

    def shard_copy(t, there, here):
        return pltpu.make_async_remote_copy(
            src_ref=shards[t],
            dst_ref=wbuf.at[t, shard_rows(here)],
            send_sem=w_send.at[t, there],
            recv_sem=w_recv.at[t, here],
            device_id={"dp": there},
            device_id_type=MESH,
        )

    def own_copy(t):
        return pltpu.make_async_copy(shards[t], wbuf.at[t, shard_rows(dp)], w_own.at[t])

    def shards_start(t):
        loop(ND - 1, lambda k: shard_copy(t, dp_peer(k), dp).start())
        own_copy(t).start()

    def shards_wait(t):
        def body(k):
            p = dp_peer(k)
            shard_copy(t, p, p).wait()

        loop(ND - 1, body)
        own_copy(t).wait()

    dispatch(0, tok, None)
    pl.semaphore_wait(bar, NE - 1 + ND - 1)
    rows_start(0)
    shards_start(0)
    shards_start(1)
    shards_start(2)
    r128 = iota((128, TD), 0)
    weights = 0.0
    for k in range(2):
        a = (hot[k] * gates[k : k + 1, :]).astype(bf16)
        weights = weights + nt(a, flag(r128 == slots[k]))
    dispatch(1, grd, weights.astype(bf16))
    rows_start(1)

    def receive(buf, dst):
        def body(n):
            both = nn(unfold[...], recv[buf, :, lanes(n)]).astype(bf16)
            dst[0:256, lanes(n)] = both[0:256]
            dst[0:256, lanes(n, start=H)] = both[256:512]

        loop(H // 256, body)
        for j, part in enumerate(tail_from_block(buf)):
            dst[256:ROWS, j * 128 : (j + 1) * 128] = part

    rows_wait(0)
    receive(0, x)
    low = nt(x[...], jnp.concatenate([gfT[...], ufT[...]], axis=0)).astype(bf16)
    gate_low, up_low = low[:, 0:16], low[:, 16:32]
    shards_wait(0)
    shards_wait(1)

    def forward(n):
        c = lanes(n)
        pre = nn(x[...], wbuf[0, :, c]) + SCALE * nn(gate_low, gs[:, c])
        up = nn(x[...], wbuf[1, :, c]) + SCALE * nn(up_low, us[:, c])
        s = jax.nn.sigmoid(pre)
        a = pre * s
        act[:, c] = a
        coef[:, c] = up * s * (1.0 + pre * (1.0 - s))
        hid[:, c] = (a * up).astype(bf16)

    loop(F // 256, forward)
    hidden_low = nt(hid[...], dfT[...]).astype(bf16)

    rows_wait(1)
    receive(1, g)
    wt = nn(take_weight, recv[1, :, H + 128 : BW])
    p256 = iota((256, 128), 0)
    l256 = iota((256, 128), 1)
    spread = flag(iota((256, NE), 0) // 8 == iota((256, NE), 1))
    gather = flag(iota((NE, 256), 1) // 8 == iota((NE, 256), 0))
    diag = l256 == p256 % 8
    ninth = iota((NE, 128), 1) == 8
    w_main = jnp.sum(jnp.where(diag, nn(spread, wt.astype(bf16)), 0.0), axis=1, keepdims=True)
    w_nine = jnp.sum(jnp.where(ninth, wt, 0.0), axis=1, keepdims=True)
    weight = jnp.concatenate([w_main, w_nine], axis=0)
    u_low = nt(g[...], dsec[...])
    cot_low = (weight * u_low).astype(bf16)
    shards_wait(2)
    sg0 = SCALE * jnp.sum(hidden_low.astype(f32) * u_low, axis=1, keepdims=True)
    bgl = jnp.zeros((ROWS, 16), f32)
    bul = jnp.zeros((ROWS, 16), f32)

    def backward(n, carry):
        slot_gate, bg, bu = carry
        c = lanes(n)
        u = nn(g[...], wbuf[2, :, c])
        slot_gate = slot_gate + jnp.sum(hid[:, c].astype(f32) * u, axis=1, keepdims=True)
        hg = weight * u + SCALE * nn(cot_low, dfT[:, c])
        gg = (hg * coef[:, c]).astype(bf16)
        ug = (hg * act[:, c]).astype(bf16)
        ggp[:, c] = gg
        ugp[:, c] = ug
        return slot_gate, bg + nt(gg, gs[:, c]), bu + nt(ug, us[:, c])

    slot_gate, bgl, bul = lax.fori_loop(0, F // 256, backward, (sg0, bgl, bul))
    bgl = bgl.astype(bf16)
    bul = bul.astype(bf16)

    def slot_grad(n):
        c = pl.ds(pl.multiple_of(n * 256, 256), 256)
        value = nt(ggp[...], wbuf[0, c, :]) + nt(ugp[...], wbuf[1, c, :])
        value = value + SCALE * (nn(bgl, gfT[:, c]) + nn(bul, ufT[:, c]))
        sg[:, c] = value.astype(bf16)

    loop(D // 256, slot_grad)

    rows_sent(0)

    def pack(n):
        both = jnp.concatenate([sg[0:256, lanes(n)], sg[0:256, lanes(n, start=H)]], axis=0)
        send[2, :, lanes(n)] = nn(fold[...], both).astype(bf16)

    loop(H // 256, pack)
    back = nn(gather, jnp.where(diag, slot_gate[0:256], 0.0).astype(bf16))
    back = back + jnp.where(ninth, slot_gate[256:ROWS], 0.0)
    tail_to_block(2, sg[256:ROWS, :], back.astype(bf16))
    rows_start(2)

    bl = jnp.concatenate([bgl, bul], axis=1)

    def store4(first, value):
        for j in range(4):
            ad_send[first + j] = value[:, j * 640 : (j + 1) * 640]

    ins = (SCALE * tn(bl, x[...])).astype(bf16)
    store4(0, ins[0:16])
    store4(4, ins[16:32])
    whl = (weight * hidden_low.astype(f32)).astype(bf16)
    store4(8, (SCALE * tn(whl, g[...])).astype(bf16))
    store4(12, jnp.concatenate([
        (SCALE * tn(gate_low, ggp[...])).astype(bf16),
        (SCALE * tn(up_low, ugp[...])).astype(bf16),
        (SCALE * tn(cot_low, hid[...])).astype(bf16),
        jnp.zeros((16, 256), bf16),
    ], axis=1))

    def part_copy(phase, there, here):
        if phase == 0:
            src, dst = ad_send.at[there], ad_recv.at[here]
        else:
            src, dst = ad_one, ad_all.at[here]
        return pltpu.make_async_remote_copy(
            src_ref=src,
            dst_ref=dst,
            send_sem=a_send.at[phase, there],
            recv_sem=a_recv.at[phase, here],
            device_id={"dp": there},
            device_id_type=MESH,
        )

    def part_wait(phase):
        def body(k):
            p = dp_peer(k)
            part_copy(phase, p, p).wait()

        loop(ND - 1, body)

    loop(ND - 1, lambda k: part_copy(0, dp_peer(k), dp).start())
    ad_recv[dp] = ad_send[dp]
    part_wait(0)
    total = lax.fori_loop(
        1, ND, lambda j, t: t + ad_recv[j].astype(f32), ad_recv[0].astype(f32)
    ).astype(bf16)
    ad_one[...] = total
    loop(ND - 1, lambda k: part_copy(1, dp_peer(k), dp).start())
    ad_all[dp] = total
    part_wait(1)

    def load4(first):
        return jnp.concatenate([ad_all[first + j].astype(f32) for j in range(4)], axis=1)

    ggi[...] = load4(0)
    gui[...] = load4(4)
    gdo[...] = load4(8)
    rest = load4(12)
    ggo[...] = rest[:, 0:F]
    guo[...] = rest[:, F : 2 * F]
    gdi[...] = rest[:, 2 * F : 3 * F]

    rows_sent(1)
    rows_sent(2)
    rows_wait(2)
    nine = jnp.concatenate(tail_from_block(2), axis=1)
    sg[0:NE, :] = nine

    def combine(n):
        r = recv[2, :, lanes(n)]
        left = tn(sel[:, 0:TD], r) + tn(sel9, sg[0:NE, lanes(n)])
        right = tn(sel[:, TD : 2 * TD], r) + tn(sel9, sg[0:NE, lanes(n, start=H)])
        tg_out[:, lanes(n)] = left.astype(bf16)
        tg_out[:, lanes(n, start=H)] = right.astype(bf16)

    loop(H // 256, combine)
    wt3 = nn(take_weight, recv[2, :, H + 128 : BW]).astype(bf16)
    for k in range(2):
        picked = tn(wt3, hot[k].astype(bf16))
        gg_out[k : k + 1, :] = jnp.sum(
            jnp.where(r128 == slots[k], picked, 0.0), axis=0, keepdims=True
        )


def per_device(tokens, out_grad, expert_ids, gate_values, wg, wu, wd, gf, gs, uf, us, df, ds):
    vmem = pl.BlockSpec(memory_space=pltpu.VMEM)
    anywhere = pl.BlockSpec(memory_space=pl.ANY)
    shape = jax.ShapeDtypeStruct
    outs = pl.pallas_call(
        kernel,
        out_shape=(
            shape((TD, D), bf16),
            shape((2, TD), f32),
            shape((16, D), f32),
            shape((16, F), f32),
            shape((16, D), f32),
            shape((16, F), f32),
            shape((16, F), f32),
            shape((16, D), f32),
        ),
        in_specs=[vmem] * 4 + [anywhere] * 3 + [vmem] * 6,
        out_specs=[vmem] * 8,
        scratch_shapes=[
            pltpu.VMEM((3, 512, BW), bf16),
            pltpu.VMEM((3, 512, BW), bf16),
            pltpu.VMEM((3, D, F), bf16),
            pltpu.VMEM((512, 2 * TD), bf16),
            pltpu.VMEM((512, 512), bf16),
            pltpu.VMEM((512, 512), bf16),
            pltpu.VMEM((512, 512), bf16),
            pltpu.VMEM((512, 512), bf16),
            pltpu.VMEM((ROWS, D), bf16),
            pltpu.VMEM((ROWS, D), bf16),
            pltpu.VMEM((ROWS, D), bf16),
            pltpu.VMEM((ROWS, F), f32),
            pltpu.VMEM((ROWS, F), f32),
            pltpu.VMEM((ROWS, F), bf16),
            pltpu.VMEM((ROWS, F), bf16),
            pltpu.VMEM((ROWS, F), bf16),
            pltpu.VMEM((16, 16, 640), bf16),
            pltpu.VMEM((16, 16, 640), bf16),
            pltpu.VMEM((16, 640), bf16),
            pltpu.VMEM((16, 16, 640), bf16),
            pltpu.SemaphoreType.DMA((3, NE)),
            pltpu.SemaphoreType.DMA((3, NE)),
            pltpu.SemaphoreType.DMA((3, ND)),
            pltpu.SemaphoreType.DMA((3, ND)),
            pltpu.SemaphoreType.DMA((3,)),
            pltpu.SemaphoreType.DMA((2, ND)),
            pltpu.SemaphoreType.DMA((2, ND)),
        ],
        compiler_params=pltpu.CompilerParams(
            collective_id=0, has_side_effects=True, vmem_limit_bytes=58 * 2**20
        ),
        cost_estimate=pl.CostEstimate(
            flops=8_000_000_000, bytes_accessed=20_000_000, transcendentals=300_000
        ),
    )(
        tokens, out_grad, expert_ids.T, gate_values.T, wg[0], wu[0], wd[0],
        gf[0].T, gs[0], uf[0].T, us[0], df[0].T, ds[0],
    )
    tg, gg, ggi, ggo, gui, guo, gdi, gdo = outs
    return tg, gg.T, ggi.T[None], ggo[None], gui.T[None], guo[None], gdi.T[None], gdo[None]


def solution(mesh):
    row = P(("dp", "expert"), None)
    frozen = P("expert", "dp", None)
    one = P("expert", None, None)
    return jax.shard_map(
        per_device,
        mesh=mesh,
        in_specs=(row,) * 4 + (frozen,) * 3 + (one,) * 6,
        out_specs=(row,) * 2 + (one,) * 6,
        check_vma=False,
    )
```

```python
import functools

import jax
import jax.numpy as jnp
from jax import lax
from jax.experimental import pallas as pl
from jax.experimental.pallas import tpu as pltpu
from jax.sharding import PartitionSpec as P

MESH = pl.DeviceIdType.MESH
bf16 = jnp.bfloat16
f32 = jnp.float32
i32 = jnp.int32

NE, ND = 32, 16
TD, D, F = 128, 2560, 768
H = D // 2
SH = D // ND
ROWS = 288
BW = H + 256
SCALE = 2.0


def nn(a, b):
    return lax.dot_general(a, b, (((1,), (0,)), ((), ())), preferred_element_type=f32)


def nt(a, b):
    return lax.dot_general(a, b, (((1,), (1,)), ((), ())), preferred_element_type=f32)


def tn(a, b):
    return lax.dot_general(a, b, (((0,), (0,)), ((), ())), preferred_element_type=f32)


def iota(shape, axis):
    return lax.broadcasted_iota(i32, shape, axis)


def flag(mask):
    return jnp.where(mask, 1.0, 0.0).astype(bf16)


def loop(n, body):
    def step(k, carry):
        body(k)
        return carry

    lax.fori_loop(0, n, step, 0)


def lanes(n, width=256, start=0):
    return pl.ds(pl.multiple_of(n * width + start, 128), width)


def kernel(
    tok, grd, ids, gates, wg, wu, wd, in_gf, in_gs, in_uf, in_us, in_df, in_ds,
    tg_out, gg_out, ggi, ggo, gui, guo, gdi, gdo,
    send, recv, wbuf, sel, perm, permT, fold, unfold, x, g, sg, coef, act, hid, ggp, ugp,
    ad_send, ad_recv, ad_one, ad_all, ad_far, ad_near,
    gfT, ufT, dsec, gs, us, dfT, moved, packed, ad_moved, ad_buf,
    s_send, s_recv, m_send, m_recv, x_send, x_recv, x_own,
    y1_send, y1_recv, y2_send, y2_recv, a_send, a_recv, f_send, f_recv,
):
    me = lax.axis_index("expert")
    dp = lax.axis_index("dp")

    z, c = me // 2, me % 2
    y, xx = dp // 4, dp % 4
    b = dp % 2
    odd = (b + c) % 2

    mine = ((z + 16 + b * (14 * c - 7)) % 16) * 2 + c
    my_slot = b * 16 + (3 + odd) * 2 + c
    my_k = c + 2 * b + 4 * (3 + odd)
    z_to = (z + 23 - 14 * c) % 16
    z_from = (z + 9 + 14 * c) % 16

    def home(k):
        c2, b2, j = k % 2, (k // 2) % 2, k // 4
        zp = (z + 13 + j - (b2 + c2) % 2) % 16
        expert = ((zp + 16 + b2 * (14 * c2 - 7)) % 16) * 2 + c2
        return dp - b + b2, zp * 2 + c2, expert, b * 16 + j * 2 + c

    def origin(slot):
        cs, j, bs = slot % 2, (slot % 16) // 2, slot // 16
        zs = (z + 19 - j + odd) % 16
        return dp - b + bs, zs * 2 + cs

    def dp_peer(k):
        return (dp + 1 + k) % ND

    bar = pltpu.get_barrier_semaphore()

    def greet(d, e):
        pl.semaphore_signal(
            bar, inc=1, device_id={"dp": d, "expert": e}, device_id_type=MESH)

    def greet_rows(k):
        i = (2 * b + c + 16 + 1 + k) % 36
        greet(dp - b + (i // 2) % 2, ((z + 12 + i // 4) % 16) * 2 + i % 2)

    loop(35, greet_rows)
    greet(dp, z_to * 2 + c)
    greet(dp, z_from * 2 + c)
    loop(ND - 1, lambda k: greet(dp_peer(k), me))

    q512 = iota((512, TD), 0)
    e32 = iota((NE, TD), 0)
    id0, id1 = ids[0:1, :], ids[1:2, :]
    hot = [jnp.where(e32 == id0, 1.0, 0.0), jnp.where(e32 == id1, 1.0, 0.0)]
    earlier = flag(iota((TD, TD), 0) < iota((TD, TD), 1))
    before = nn((hot[0] + hot[1]).astype(bf16), earlier)
    slots = [jnp.sum(before * h, axis=0, keepdims=True).astype(i32) for h in hot]
    keys = [
        jnp.where(slots[0] < 8, id0 * 16 + slots[0], -16),
        jnp.where(slots[1] < 8, id1 * 16 + slots[1], -16),
    ]
    sel[:, 0:TD] = flag((q512 == keys[0]) | (q512 == keys[1]))
    sel[:, TD : 2 * TD] = flag((q512 == keys[0] + 8) | (q512 == keys[1] + 8))
    sel9 = (
        jnp.where(slots[0] == 8, hot[0], 0.0) + jnp.where(slots[1] == 8, hot[1], 0.0)
    ).astype(bf16)
    qa, qb = iota((512, 512), 0), iota((512, 512), 1)
    perm[...] = flag(qb == (qa % 16) * 32 + qa // 16)
    permT[...] = flag(qa == (qb % 16) * 32 + qb // 16)
    cb = qb % 256
    fold[...] = flag(qa == (cb // 8) * 16 + cb % 8 + (qb // 256) * 8)
    ca = qa % 256
    unfold[...] = flag(qb == (ca // 8) * 16 + ca % 8 + (qa // 256) * 8)
    put_weight = flag(iota((512, NE), 0) == iota((512, NE), 1) * 16 + 4)
    take_weight = flag(iota((NE, 512), 1) == iota((NE, 512), 0) * 16 + 4)

    def tail_to_block(buf, nine, extra):
        first = jnp.concatenate([nine[:, j * 128 : (j + 1) * 128] for j in range(16)], axis=0)
        last = jnp.concatenate([nine[:, j * 128 : (j + 1) * 128] for j in range(16, 20)], axis=0)
        send[buf, :, H : H + 128] = nn(perm[...], first).astype(bf16)
        z1 = nn(perm[:, 0:128], last)
        if extra is not None:
            z1 = z1 + nn(put_weight, extra)
        send[buf, :, H + 128 : BW] = z1.astype(bf16)

    def tail_from_block(buf):
        first = nn(permT[...], recv[buf, :, H : H + 128]).astype(bf16)
        last = nn(permT[0:128, :], recv[buf, :, H + 128 : BW]).astype(bf16)
        parts = [first[j * 32 : (j + 1) * 32] for j in range(16)]
        parts += [last[j * 32 : (j + 1) * 32] for j in range(4)]
        return parts

    def dispatch(buf, src, extra):
        def body(n):
            both = jnp.concatenate([src[:, lanes(n)], src[:, lanes(n, start=H)]], axis=0)
            send[buf, :, lanes(n)] = nn(sel[...], both).astype(bf16)

        loop(H // 256, body)
        tail_to_block(buf, nn(sel9, src[...]).astype(bf16), extra)

    def block(p):
        return pl.ds(pl.multiple_of(p * 16, 16), 16)

    def row_copy(buf, src, dst, d, e):
        return pltpu.make_async_remote_copy(
            src_ref=send.at[buf, block(src)],
            dst_ref=recv.at[buf, block(dst)],
            send_sem=s_send.at[buf, src],
            recv_sem=s_recv.at[buf, dst],
            device_id={"dp": d, "expert": e},
            device_id_type=MESH,
        )

    def rows_start(buf):
        def body(i):
            d, e, expert, slot = home((my_k + 1 + i) % NE)
            row_copy(buf, expert, slot, d, e).start()

        loop(NE - 1, body)
        recv[buf, block(my_slot), :] = send[buf, block(mine), :]

    def rows_back():
        def body(i):
            slot = (my_slot + 1 + i) % NE
            d, e = origin(slot)
            row_copy(2, slot, mine, d, e).start()

        loop(NE - 1, body)
        recv[2, block(mine), :] = send[2, block(my_slot), :]

    def rows_wait(buf, own):
        loop(NE - 1, lambda i: row_copy(
            buf, (own + 1 + i) % NE, (own + 1 + i) % NE, dp, z_to * 2 + c).wait_recv())

    def rows_sent(buf, own):
        loop(NE - 1, lambda i: row_copy(
            buf, (own + 1 + i) % NE, (own + 1 + i) % NE, dp, z_to * 2 + c).wait_send())

    shards = [wg, wu, wd, packed.at[dp]]
    second = [moved.at[0], moved.at[1], moved.at[2], ad_moved]
    order = (3, 0, 1, 2)

    def shard(t, d):
        if t == 3:
            return ad_buf.at[d]
        return wbuf.at[t, pl.ds(pl.multiple_of(d * SH, 32), SH)]

    def four(t, row, part):
        if t == 3:
            return ad_buf.at[pl.ds(row * 4 + (2 if part == 2 else 0), 2 if part else 4)]
        first = row * 4 * SH + (2 * SH if part == 2 else 0)
        return wbuf.at[t, pl.ds(pl.multiple_of(first, 64), (2 if part else 4) * SH)]

    def move(t):
        return pltpu.make_async_remote_copy(
            src_ref=shards[t], dst_ref=second[t], send_sem=m_send.at[t], recv_sem=m_recv.at[t],
            device_id={"expert": z_to * 2 + c}, device_id_type=MESH,
        )

    def along_x(t, src, to, at):
        return pltpu.make_async_remote_copy(
            src_ref=src, dst_ref=shard(t, y * 4 + at),
            send_sem=x_send.at[t, to], recv_sem=x_recv.at[t, at],
            device_id={"dp": y * 4 + to}, device_id_type=MESH,
        )

    def x_start(t, stream):
        src = shards[t] if stream == 0 else second[t]

        def body(i):
            to = stream + 2 * i

            @pl.when(to != xx)
            def _():
                along_x(t, src, to, xx).start()

            @pl.when(to == xx)
            def _():
                pltpu.make_async_copy(src, shard(t, dp), x_own.at[t]).start()

        loop(2, body)

    def x_wait(t):
        loop(3, lambda i: along_x(
            t, shards[t], (xx + 1 + i) % 4, (xx + 1 + i) % 4).wait_recv())
        pltpu.make_async_copy(shards[t], shard(t, dp), x_own.at[t]).wait()

    def x_sent(t):
        loop(3, lambda i: along_x(
            t, shards[t], (xx + 1 + i) % 4, (xx + 1 + i) % 4).wait_send())

    ends = ((y + 1) % 4, (y + 3) % 4)

    def along_y(t, way, hop):
        region = four(t, y, 0) if hop == 1 else four(t, ends[1 - way], way + 1)
        sems = (y1_send, y1_recv) if hop == 1 else (y2_send, y2_recv)
        return pltpu.make_async_remote_copy(
            src_ref=region, dst_ref=region,
            send_sem=sems[0].at[t, way], recv_sem=sems[1].at[t, way],
            device_id={"dp": ends[way] * 4 + xx}, device_id_type=MESH,
        )

    def landed_y(t, way, hop):
        region = four(t, ends[1 - way], 0) if hop == 1 else four(t, (y + 2) % 4, way + 1)
        sems = (y1_send, y1_recv) if hop == 1 else (y2_send, y2_recv)
        pltpu.make_async_remote_copy(
            src_ref=region, dst_ref=region,
            send_sem=sems[0].at[t, way], recv_sem=sems[1].at[t, way],
            device_id={"dp": ends[way] * 4 + xx}, device_id_type=MESH,
        ).wait_recv()

    def move_done(t):
        move(t).wait_recv()
        x_start(t, 1)

    def y_first(t):
        x_wait(t)
        along_y(t, 0, 1).start()
        along_y(t, 1, 1).start()

    def y_second(t):
        for way in range(2):
            landed_y(t, way, 1)
            along_y(t, way, 2).start()

    def y_done(t):
        landed_y(t, 0, 2)
        landed_y(t, 1, 2)

    for first, ref in ((0, in_gf), (4, in_uf), (8, in_ds)):
        for j in range(4):
            packed[first + j] = ref[:, j * 640 : (j + 1) * 640]
    small = jnp.concatenate(
        [in_gs[...], in_us[...], in_df[...], jnp.zeros((16, 256), bf16)], axis=1
    )
    for j in range(4):
        packed[12 + j] = small[:, j * 640 : (j + 1) * 640]

    dispatch(0, tok, None)
    pl.semaphore_wait(bar, 35 + 2 + ND - 1)
    for t in order:
        move(t).start()
    for t in order:
        x_start(t, 0)
    rows_start(0)
    r128 = iota((128, TD), 0)
    weights = 0.0
    for k in range(2):
        a = (hot[k] * gates[k : k + 1, :]).astype(bf16)
        weights = weights + nt(a, flag(r128 == slots[k]))
    dispatch(1, grd, weights.astype(bf16))
    rows_start(1)

    move_done(3)
    move_done(0)
    y_first(3)
    y_first(0)
    move_done(1)
    y_first(1)
    y_second(3)
    y_second(0)
    move_done(2)
    y_first(2)
    y_second(1)

    def receive(buf, dst):
        def body(n):
            both = nn(unfold[...], recv[buf, :, lanes(n)]).astype(bf16)
            dst[0:256, lanes(n)] = both[0:256]
            dst[0:256, lanes(n, start=H)] = both[256:512]

        loop(H // 256, body)
        for j, part in enumerate(tail_from_block(buf)):
            dst[256:ROWS, j * 128 : (j + 1) * 128] = part

    rows_wait(0, my_slot)
    receive(0, x)
    y_done(3)

    def load4(buf, first):
        return jnp.concatenate([buf[first + j] for j in range(4)], axis=1)

    gfT[...] = load4(ad_buf, 0)
    ufT[...] = load4(ad_buf, 4)
    dsec[...] = load4(ad_buf, 8)
    rest = load4(ad_buf, 12)
    gs[...] = rest[:, 0:F]
    us[...] = rest[:, F : 2 * F]
    dfT[...] = rest[:, 2 * F : 3 * F]
    low = nt(x[...], jnp.concatenate([gfT[...], ufT[...]], axis=0)).astype(bf16)
    gate_low, up_low = low[:, 0:16], low[:, 16:32]
    y_second(2)
    y_done(0)
    y_done(1)

    def forward(n):
        c = lanes(n)
        pre = nn(x[...], wbuf[0, :, c]) + SCALE * nn(gate_low, gs[:, c])
        up = nn(x[...], wbuf[1, :, c]) + SCALE * nn(up_low, us[:, c])
        s = jax.nn.sigmoid(pre)
        a = pre * s
        act[:, c] = a
        coef[:, c] = up * s * (1.0 + pre * (1.0 - s))
        hid[:, c] = (a * up).astype(bf16)

    loop(F // 256, forward)
    hidden_low = nt(hid[...], dfT[...]).astype(bf16)

    rows_wait(1, my_slot)
    receive(1, g)
    wt = nn(take_weight, recv[1, :, H + 128 : BW])
    p256 = iota((256, 128), 0)
    l256 = iota((256, 128), 1)
    spread = flag(iota((256, NE), 0) // 8 == iota((256, NE), 1))
    gather = flag(iota((NE, 256), 1) // 8 == iota((NE, 256), 0))
    diag = l256 == p256 % 8
    ninth = iota((NE, 128), 1) == 8
    w_main = jnp.sum(jnp.where(diag, nn(spread, wt.astype(bf16)), 0.0), axis=1, keepdims=True)
    w_nine = jnp.sum(jnp.where(ninth, wt, 0.0), axis=1, keepdims=True)
    weight = jnp.concatenate([w_main, w_nine], axis=0)
    u_low = nt(g[...], dsec[...])
    cot_low = (weight * u_low).astype(bf16)
    y_done(2)
    sg0 = SCALE * jnp.sum(hidden_low.astype(f32) * u_low, axis=1, keepdims=True)
    bgl = jnp.zeros((ROWS, 16), f32)
    bul = jnp.zeros((ROWS, 16), f32)

    def backward(n, carry):
        slot_gate, bg, bu = carry
        c = lanes(n)
        u = nn(g[...], wbuf[2, :, c])
        slot_gate = slot_gate + jnp.sum(hid[:, c].astype(f32) * u, axis=1, keepdims=True)
        hg = weight * u + SCALE * nn(cot_low, dfT[:, c])
        gg = (hg * coef[:, c]).astype(bf16)
        ug = (hg * act[:, c]).astype(bf16)
        ggp[:, c] = gg
        ugp[:, c] = ug
        return slot_gate, bg + nt(gg, gs[:, c]), bu + nt(ug, us[:, c])

    slot_gate, bgl, bul = lax.fori_loop(0, F // 256, backward, (sg0, bgl, bul))
    bgl = bgl.astype(bf16)
    bul = bul.astype(bf16)

    def slot_grad(n):
        c = pl.ds(pl.multiple_of(n * 256, 256), 256)
        value = nt(ggp[...], wbuf[0, c, :]) + nt(ugp[...], wbuf[1, c, :])
        value = value + SCALE * (nn(bgl, gfT[:, c]) + nn(bul, ufT[:, c]))
        sg[:, c] = value.astype(bf16)

    loop(D // 256, slot_grad)

    def pack(n):
        both = jnp.concatenate([sg[0:256, lanes(n)], sg[0:256, lanes(n, start=H)]], axis=0)
        send[2, :, lanes(n)] = nn(fold[...], both).astype(bf16)

    loop(H // 256, pack)
    back = nn(gather, jnp.where(diag, slot_gate[0:256], 0.0).astype(bf16))
    back = back + jnp.where(ninth, slot_gate[256:ROWS], 0.0)
    tail_to_block(2, sg[256:ROWS, :], back.astype(bf16))
    rows_back()

    bl = jnp.concatenate([bgl, bul], axis=1)

    def store4(first, value):
        for j in range(4):
            ad_send[first + j] = value[:, j * 640 : (j + 1) * 640]

    ins = (SCALE * tn(bl, x[...])).astype(bf16)
    store4(0, ins[0:16])
    store4(4, ins[16:32])
    whl = (weight * hidden_low.astype(f32)).astype(bf16)
    store4(8, (SCALE * tn(whl, g[...])).astype(bf16))
    store4(12, jnp.concatenate([
        (SCALE * tn(gate_low, ggp[...])).astype(bf16),
        (SCALE * tn(up_low, ugp[...])).astype(bf16),
        (SCALE * tn(cot_low, hid[...])).astype(bf16),
        jnp.zeros((16, 256), bf16),
    ], axis=1))

    def part_copy(phase, there, here):
        if phase == 0:
            src, dst = ad_send.at[there], ad_recv.at[here]
        else:
            src, dst = ad_one, ad_all.at[here]
        return pltpu.make_async_remote_copy(
            src_ref=src,
            dst_ref=dst,
            send_sem=a_send.at[phase, there],
            recv_sem=a_recv.at[phase, here],
            device_id={"dp": there},
            device_id_type=MESH,
        )

    def part_wait(phase):
        def body(k):
            p = dp_peer(k)
            part_copy(phase, p, p).wait()

        loop(ND - 1, body)

    loop(ND - 1, lambda k: part_copy(0, dp_peer(k), dp).start())
    ad_recv[dp] = ad_send[dp]
    part_wait(0)

    def both(j, t):
        return t[0] + ad_recv[2 * j].astype(f32), t[1] + ad_recv[2 * j + 1].astype(f32)

    zero = jnp.zeros((16, 640), f32)
    here, there = lax.fori_loop(0, ND // 2, both, (zero, zero))
    ad_far[...] = there
    far = pltpu.make_async_remote_copy(
        src_ref=ad_far, dst_ref=ad_near, send_sem=f_send.at[0], recv_sem=f_recv.at[0],
        device_id={"expert": z_from * 2 + c}, device_id_type=MESH,
    )
    far.start()
    far.wait()
    total = (here + ad_near[...]).astype(bf16)
    ad_one[...] = total
    loop(ND - 1, lambda k: part_copy(1, dp_peer(k), dp).start())
    ad_all[dp] = total
    part_wait(1)

    ggi[...] = load4(ad_all, 0).astype(f32)
    gui[...] = load4(ad_all, 4).astype(f32)
    gdo[...] = load4(ad_all, 8).astype(f32)
    rest = load4(ad_all, 12).astype(f32)
    ggo[...] = rest[:, 0:F]
    guo[...] = rest[:, F : 2 * F]
    gdi[...] = rest[:, 2 * F : 3 * F]

    for t in order:
        move(t).wait_send()
        x_sent(t)
        for way in range(2):
            along_y(t, way, 1).wait_send()
            along_y(t, way, 2).wait_send()
    rows_sent(0, mine)
    rows_sent(1, mine)
    rows_sent(2, my_slot)
    rows_wait(2, mine)
    nine = jnp.concatenate(tail_from_block(2), axis=1)
    sg[0:NE, :] = nine

    def combine(n):
        r = recv[2, :, lanes(n)]
        left = tn(sel[:, 0:TD], r) + tn(sel9, sg[0:NE, lanes(n)])
        right = tn(sel[:, TD : 2 * TD], r) + tn(sel9, sg[0:NE, lanes(n, start=H)])
        tg_out[:, lanes(n)] = left.astype(bf16)
        tg_out[:, lanes(n, start=H)] = right.astype(bf16)

    loop(H // 256, combine)
    wt3 = nn(take_weight, recv[2, :, H + 128 : BW]).astype(bf16)
    for k in range(2):
        picked = tn(wt3, hot[k].astype(bf16))
        gg_out[k : k + 1, :] = jnp.sum(
            jnp.where(r128 == slots[k], picked, 0.0), axis=0, keepdims=True
        )


def per_device(tokens, out_grad, expert_ids, gate_values, wg, wu, wd, gf, gs, uf, us, df, ds):
    vmem = pl.BlockSpec(memory_space=pltpu.VMEM)
    anywhere = pl.BlockSpec(memory_space=pl.ANY)
    shape = jax.ShapeDtypeStruct
    outs = pl.pallas_call(
        kernel,
        out_shape=(
            shape((TD, D), bf16),
            shape((2, TD), f32),
            shape((16, D), f32),
            shape((16, F), f32),
            shape((16, D), f32),
            shape((16, F), f32),
            shape((16, F), f32),
            shape((16, D), f32),
        ),
        in_specs=[vmem] * 4 + [anywhere] * 3 + [vmem] * 6,
        out_specs=[vmem] * 8,
        scratch_shapes=[
            pltpu.VMEM((3, 512, BW), bf16),
            pltpu.VMEM((3, 512, BW), bf16),
            pltpu.VMEM((3, D, F), bf16),
            pltpu.VMEM((512, 2 * TD), bf16),
            pltpu.VMEM((512, 512), bf16),
            pltpu.VMEM((512, 512), bf16),
            pltpu.VMEM((512, 512), bf16),
            pltpu.VMEM((512, 512), bf16),
            pltpu.VMEM((ROWS, D), bf16),
            pltpu.VMEM((ROWS, D), bf16),
            pltpu.VMEM((ROWS, D), bf16),
            pltpu.VMEM((ROWS, F), f32),
            pltpu.VMEM((ROWS, F), f32),
            pltpu.VMEM((ROWS, F), bf16),
            pltpu.VMEM((ROWS, F), bf16),
            pltpu.VMEM((ROWS, F), bf16),
            pltpu.VMEM((16, 16, 640), bf16),
            pltpu.VMEM((16, 16, 640), bf16),
            pltpu.VMEM((16, 640), bf16),
            pltpu.VMEM((16, 16, 640), bf16),
            pltpu.VMEM((16, 640), f32),
            pltpu.VMEM((16, 640), f32),
            pltpu.VMEM((16, D), bf16),
            pltpu.VMEM((16, D), bf16),
            pltpu.VMEM((16, D), bf16),
            pltpu.VMEM((16, F), bf16),
            pltpu.VMEM((16, F), bf16),
            pltpu.VMEM((16, F), bf16),
            pltpu.VMEM((3, SH, F), bf16),
            pltpu.VMEM((16, 16, 640), bf16),
            pltpu.VMEM((16, 640), bf16),
            pltpu.VMEM((16, 16, 640), bf16),
            pltpu.SemaphoreType.DMA((3, NE)),
            pltpu.SemaphoreType.DMA((3, NE)),
            pltpu.SemaphoreType.DMA((4,)),
            pltpu.SemaphoreType.DMA((4,)),
            pltpu.SemaphoreType.DMA((4, 4)),
            pltpu.SemaphoreType.DMA((4, 4)),
            pltpu.SemaphoreType.DMA((4,)),
            pltpu.SemaphoreType.DMA((4, 2)),
            pltpu.SemaphoreType.DMA((4, 2)),
            pltpu.SemaphoreType.DMA((4, 2)),
            pltpu.SemaphoreType.DMA((4, 2)),
            pltpu.SemaphoreType.DMA((2, ND)),
            pltpu.SemaphoreType.DMA((2, ND)),
            pltpu.SemaphoreType.DMA((1,)),
            pltpu.SemaphoreType.DMA((1,)),
        ],
        compiler_params=pltpu.CompilerParams(
            collective_id=0, has_side_effects=True, vmem_limit_bytes=58 * 2**20
        ),
        cost_estimate=pl.CostEstimate(
            flops=8_000_000_000, bytes_accessed=20_000_000, transcendentals=300_000
        ),
    )(
        tokens, out_grad, expert_ids.T, gate_values.T, wg[0], wu[0], wd[0],
        gf[0].T, gs[0], uf[0].T, us[0], df[0].T, ds[0],
    )
    tg, gg, ggi, ggo, gui, guo, gdi, gdo = outs
    return tg, gg.T, ggi.T[None], ggo[None], gui.T[None], guo[None], gdi.T[None], gdo[None]


def solution(mesh):
    row = P(("dp", "expert"), None)
    frozen = P("expert", "dp", None)
    one = P("expert", None, None)
    return jax.shard_map(
        per_device,
        mesh=mesh,
        in_specs=(row,) * 4 + (frozen,) * 3 + (one,) * 6,
        out_specs=(row,) * 2 + (one,) * 6,
        check_vma=False,
    )
```

```python
import functools

import jax
import jax.numpy as jnp
from jax import lax
from jax.experimental import pallas as pl
from jax.experimental.pallas import tpu as pltpu
from jax.sharding import PartitionSpec as P

MESH = pl.DeviceIdType.MESH
bf16 = jnp.bfloat16
f32 = jnp.float32
i32 = jnp.int32

NE, ND = 32, 16
TD, D, F = 128, 2560, 768
H = D // 2
SH = D // ND
ROWS = 288
BW = H + 256
PIECES = 9
SCALE = 2.0


def nn(a, b):
    return lax.dot_general(a, b, (((1,), (0,)), ((), ())), preferred_element_type=f32)


def nt(a, b):
    return lax.dot_general(a, b, (((1,), (1,)), ((), ())), preferred_element_type=f32)


def tn(a, b):
    return lax.dot_general(a, b, (((0,), (0,)), ((), ())), preferred_element_type=f32)


def iota(shape, axis):
    return lax.broadcasted_iota(i32, shape, axis)


def flag(mask):
    return jnp.where(mask, 1.0, 0.0).astype(bf16)


def loop(n, body):
    def step(k, carry):
        body(k)
        return carry

    lax.fori_loop(0, n, step, 0)


def lanes(n, width=256, start=0):
    return pl.ds(pl.multiple_of(n * width + start, 128), width)


def kernel(
    tok, grd, ids, gates, wg, wu, wd, in_gf, in_gs, in_uf, in_us, in_df, in_ds,
    tg_out, gg_out, ggi, ggo, gui, guo, gdi, gdo,
    send, recv, wbuf, sel, perm, permT, fold, unfold, x, g, sg, coef, act, hid, ggp, ugp,
    ad_send, ad_recv, ad_one, ad_all, ad_far, ad_near,
    gfT, ufT, dsec, gs, us, dfT, staged, moved, packed, ad_moved, ad_buf,
    s_send, s_recv, st_sem, m_send, m_recv, x_send, x_recv, x_own,
    y1_send, y1_recv, y2_send, y2_recv, a_send, a_recv, f_send, f_recv,
):
    me = lax.axis_index("expert")
    dp = lax.axis_index("dp")

    z, c = me // 2, me % 2
    y, xx = dp // 4, dp % 4
    b = dp % 2
    odd = (b + c) % 2

    mine = ((z + 16 + b * (14 * c - 7)) % 16) * 2 + c
    my_slot = b * 16 + (3 + odd) * 2 + c
    my_k = c + 2 * b + 4 * (3 + odd)
    z_to = (z + 23 - 14 * c) % 16
    z_from = (z + 9 + 14 * c) % 16

    def home(k):
        c2, b2, j = k % 2, (k // 2) % 2, k // 4
        zp = (z + 13 + j - (b2 + c2) % 2) % 16
        expert = ((zp + 16 + b2 * (14 * c2 - 7)) % 16) * 2 + c2
        return dp - b + b2, zp * 2 + c2, expert, b * 16 + j * 2 + c

    def origin(slot):
        cs, j, bs = slot % 2, (slot % 16) // 2, slot // 16
        zs = (z + 19 - j + odd) % 16
        return dp - b + bs, zs * 2 + cs

    def dp_peer(k):
        return (dp + 1 + k) % ND

    bar = pltpu.get_barrier_semaphore()

    def greet(d, e):
        pl.semaphore_signal(
            bar, inc=1, device_id={"dp": d, "expert": e}, device_id_type=MESH)

    def greet_rows(k):
        i = (2 * b + c + 16 + 1 + k) % 36
        greet(dp - b + (i // 2) % 2, ((z + 12 + i // 4) % 16) * 2 + i % 2)

    loop(35, greet_rows)
    greet(dp, z_to * 2 + c)
    greet(dp, z_from * 2 + c)
    loop(ND - 1, lambda k: greet(dp_peer(k), me))

    q512 = iota((512, TD), 0)
    e32 = iota((NE, TD), 0)
    id0, id1 = ids[0:1, :], ids[1:2, :]
    hot = [jnp.where(e32 == id0, 1.0, 0.0), jnp.where(e32 == id1, 1.0, 0.0)]
    earlier = flag(iota((TD, TD), 0) < iota((TD, TD), 1))
    before = nn((hot[0] + hot[1]).astype(bf16), earlier)
    slots = [jnp.sum(before * h, axis=0, keepdims=True).astype(i32) for h in hot]
    keys = [
        jnp.where(slots[0] < 8, id0 * 16 + slots[0], -16),
        jnp.where(slots[1] < 8, id1 * 16 + slots[1], -16),
    ]
    sel[:, 0:TD] = flag((q512 == keys[0]) | (q512 == keys[1]))
    sel[:, TD : 2 * TD] = flag((q512 == keys[0] + 8) | (q512 == keys[1] + 8))
    sel9 = (
        jnp.where(slots[0] == 8, hot[0], 0.0) + jnp.where(slots[1] == 8, hot[1], 0.0)
    ).astype(bf16)
    qa, qb = iota((512, 512), 0), iota((512, 512), 1)
    perm[...] = flag(qb == (qa % 16) * 32 + qa // 16)
    permT[...] = flag(qa == (qb % 16) * 32 + qb // 16)
    cb = qb % 256
    fold[...] = flag(qa == (cb // 8) * 16 + cb % 8 + (qb // 256) * 8)
    ca = qa % 256
    unfold[...] = flag(qb == (ca // 8) * 16 + ca % 8 + (qa // 256) * 8)
    put_weight = flag(iota((512, NE), 0) == iota((512, NE), 1) * 16 + 4)
    take_weight = flag(iota((NE, 512), 1) == iota((NE, 512), 0) * 16 + 4)

    def tail_to_block(buf, nine, extra):
        first = jnp.concatenate([nine[:, j * 128 : (j + 1) * 128] for j in range(16)], axis=0)
        last = jnp.concatenate([nine[:, j * 128 : (j + 1) * 128] for j in range(16, 20)], axis=0)
        send[buf, :, H : H + 128] = nn(perm[...], first).astype(bf16)
        z1 = nn(perm[:, 0:128], last)
        if extra is not None:
            z1 = z1 + nn(put_weight, extra)
        send[buf, :, H + 128 : BW] = z1.astype(bf16)

    def tail_from_block(buf):
        first = nn(permT[...], recv[buf, :, H : H + 128]).astype(bf16)
        last = nn(permT[0:128, :], recv[buf, :, H + 128 : BW]).astype(bf16)
        parts = [first[j * 32 : (j + 1) * 32] for j in range(16)]
        parts += [last[j * 32 : (j + 1) * 32] for j in range(4)]
        return parts

    def dispatch(buf, src, extra):
        def body(n):
            both = jnp.concatenate([src[:, lanes(n)], src[:, lanes(n, start=H)]], axis=0)
            send[buf, :, lanes(n)] = nn(sel[...], both).astype(bf16)

        loop(H // 256, body)
        tail_to_block(buf, nn(sel9, src[...]).astype(bf16), extra)

    def block(p):
        return pl.ds(pl.multiple_of(p * 16, 16), 16)

    def row_copy(buf, src, dst, d, e):
        return pltpu.make_async_remote_copy(
            src_ref=send.at[buf, block(src)],
            dst_ref=recv.at[buf, block(dst)],
            send_sem=s_send.at[buf, src],
            recv_sem=s_recv.at[buf, dst],
            device_id={"dp": d, "expert": e},
            device_id_type=MESH,
        )

    def rows_start(buf):
        def body(i):
            d, e, expert, slot = home((my_k + 1 + i) % NE)
            row_copy(buf, expert, slot, d, e).start()

        loop(NE - 1, body)
        recv[buf, block(my_slot), :] = send[buf, block(mine), :]

    def rows_back():
        def body(i):
            slot = (my_slot + 1 + i) % NE
            d, e = origin(slot)
            row_copy(2, slot, mine, d, e).start()

        loop(NE - 1, body)
        recv[2, block(mine), :] = send[2, block(my_slot), :]

    def rows_wait(buf, own):
        loop(NE - 1, lambda i: row_copy(
            buf, (own + 1 + i) % NE, (own + 1 + i) % NE, dp, z_to * 2 + c).wait_recv())

    def rows_sent(buf, own):
        loop(NE - 1, lambda i: row_copy(
            buf, (own + 1 + i) % NE, (own + 1 + i) % NE, dp, z_to * 2 + c).wait_send())

    AD = PIECES

    def stage(t):
        ref, n = ((wg, wu)[t % 2], t // 2) if t < 6 else (wd, t - 6)
        return pltpu.make_async_copy(
            ref.at[:, n * 256 : (n + 1) * 256], staged.at[t], st_sem.at[t])

    for t in range(PIECES):
        stage(t).start()

    def is_ad(t):
        return isinstance(t, int) and t == AD

    def first_of(t):
        return packed.at[dp] if is_ad(t) else staged.at[t]

    def second_of(t):
        return ad_moved if is_ad(t) else moved.at[t]

    def shard(t, d):
        if is_ad(t):
            return ad_buf.at[d]
        return wbuf.at[t, pl.ds(pl.multiple_of(d * SH, 32), SH)]

    def four(t, row, part):
        if is_ad(t):
            return ad_buf.at[pl.ds(row * 4 + (2 if part == 2 else 0), 2 if part else 4)]
        first = row * 4 * SH + (2 * SH if part == 2 else 0)
        return wbuf.at[t, pl.ds(pl.multiple_of(first, 64), (2 if part else 4) * SH)]

    def move(t):
        return pltpu.make_async_remote_copy(
            src_ref=first_of(t), dst_ref=second_of(t), send_sem=m_send.at[t], recv_sem=m_recv.at[t],
            device_id={"expert": z_to * 2 + c}, device_id_type=MESH,
        )

    def along_x(t, src, to, at):
        return pltpu.make_async_remote_copy(
            src_ref=src, dst_ref=shard(t, y * 4 + at),
            send_sem=x_send.at[t, to], recv_sem=x_recv.at[t, at],
            device_id={"dp": y * 4 + to}, device_id_type=MESH,
        )

    def x_start(t, stream):
        src = first_of(t) if stream == 0 else second_of(t)

        def body(i):
            to = stream + 2 * i

            @pl.when(to != xx)
            def _():
                along_x(t, src, to, xx).start()

            @pl.when(to == xx)
            def _():
                pltpu.make_async_copy(src, shard(t, dp), x_own.at[t]).start()

        loop(2, body)

    def x_wait(t):
        loop(3, lambda i: along_x(
            t, first_of(t), (xx + 1 + i) % 4, (xx + 1 + i) % 4).wait_recv())
        pltpu.make_async_copy(first_of(t), shard(t, dp), x_own.at[t]).wait()

    def x_sent(t):
        loop(3, lambda i: along_x(
            t, first_of(t), (xx + 1 + i) % 4, (xx + 1 + i) % 4).wait_send())

    ends = ((y + 1) % 4, (y + 3) % 4)

    def along_y(t, way, hop):
        region = four(t, y, 0) if hop == 1 else four(t, ends[1 - way], way + 1)
        sems = (y1_send, y1_recv) if hop == 1 else (y2_send, y2_recv)
        return pltpu.make_async_remote_copy(
            src_ref=region, dst_ref=region,
            send_sem=sems[0].at[t, way], recv_sem=sems[1].at[t, way],
            device_id={"dp": ends[way] * 4 + xx}, device_id_type=MESH,
        )

    def landed_y(t, way, hop):
        region = four(t, ends[1 - way], 0) if hop == 1 else four(t, (y + 2) % 4, way + 1)
        sems = (y1_send, y1_recv) if hop == 1 else (y2_send, y2_recv)
        pltpu.make_async_remote_copy(
            src_ref=region, dst_ref=region,
            send_sem=sems[0].at[t, way], recv_sem=sems[1].at[t, way],
            device_id={"dp": ends[way] * 4 + xx}, device_id_type=MESH,
        ).wait_recv()

    def move_done(t):
        move(t).wait_recv()
        x_start(t, 1)

    def y_first(t):
        x_wait(t)
        along_y(t, 0, 1).start()
        along_y(t, 1, 1).start()

    def y_second(t):
        for way in range(2):
            landed_y(t, way, 1)
            along_y(t, way, 2).start()

    def y_done(t):
        landed_y(t, 0, 2)
        landed_y(t, 1, 2)

    for first, ref in ((0, in_gf), (4, in_uf), (8, in_ds)):
        for j in range(4):
            packed[first + j] = ref[:, j * 640 : (j + 1) * 640]
    small = jnp.concatenate(
        [in_gs[...], in_us[...], in_df[...], jnp.zeros((16, 256), bf16)], axis=1
    )
    for j in range(4):
        packed[12 + j] = small[:, j * 640 : (j + 1) * 640]

    dispatch(0, tok, None)
    pl.semaphore_wait(bar, 35 + 2 + ND - 1)
    for t in range(PIECES):
        stage(t).wait()
    move(AD).start()
    loop(PIECES, lambda t: move(t).start())
    x_start(AD, 0)
    loop(PIECES, lambda t: x_start(t, 0))
    rows_start(0)
    r128 = iota((128, TD), 0)
    weights = 0.0
    for k in range(2):
        a = (hot[k] * gates[k : k + 1, :]).astype(bf16)
        weights = weights + nt(a, flag(r128 == slots[k]))
    dispatch(1, grd, weights.astype(bf16))
    rows_start(1)

    move_done(AD)
    move_done(0)
    y_first(AD)
    move_done(1)
    y_first(0)
    y_second(AD)

    def relay(i):
        move_done(i + 2)
        y_first(i + 1)
        y_second(i)

    loop(PIECES - 2, relay)
    y_first(PIECES - 1)

    def receive(buf, dst):
        def body(n):
            both = nn(unfold[...], recv[buf, :, lanes(n)]).astype(bf16)
            dst[0:256, lanes(n)] = both[0:256]
            dst[0:256, lanes(n, start=H)] = both[256:512]

        loop(H // 256, body)
        for j, part in enumerate(tail_from_block(buf)):
            dst[256:ROWS, j * 128 : (j + 1) * 128] = part

    rows_wait(0, my_slot)
    receive(0, x)
    y_done(AD)

    def load4(buf, first):
        return jnp.concatenate([buf[first + j] for j in range(4)], axis=1)

    gfT[...] = load4(ad_buf, 0)
    ufT[...] = load4(ad_buf, 4)
    dsec[...] = load4(ad_buf, 8)
    rest = load4(ad_buf, 12)
    gs[...] = rest[:, 0:F]
    us[...] = rest[:, F : 2 * F]
    dfT[...] = rest[:, 2 * F : 3 * F]
    low = nt(x[...], jnp.concatenate([gfT[...], ufT[...]], axis=0)).astype(bf16)
    gate_low, up_low = low[:, 0:16], low[:, 16:32]
    y_second(PIECES - 2)
    y_second(PIECES - 1)

    def forward(n):
        c = lanes(n)
        y_done(2 * n)
        pre = nn(x[...], wbuf[2 * n]) + SCALE * nn(gate_low, gs[:, c])
        y_done(2 * n + 1)
        up = nn(x[...], wbuf[2 * n + 1]) + SCALE * nn(up_low, us[:, c])
        s = jax.nn.sigmoid(pre)
        a = pre * s
        act[:, c] = a
        coef[:, c] = up * s * (1.0 + pre * (1.0 - s))
        hid[:, c] = (a * up).astype(bf16)

    loop(F // 256, forward)
    hidden_low = nt(hid[...], dfT[...]).astype(bf16)

    rows_wait(1, my_slot)
    receive(1, g)
    wt = nn(take_weight, recv[1, :, H + 128 : BW])
    p256 = iota((256, 128), 0)
    l256 = iota((256, 128), 1)
    spread = flag(iota((256, NE), 0) // 8 == iota((256, NE), 1))
    gather = flag(iota((NE, 256), 1) // 8 == iota((NE, 256), 0))
    diag = l256 == p256 % 8
    ninth = iota((NE, 128), 1) == 8
    w_main = jnp.sum(jnp.where(diag, nn(spread, wt.astype(bf16)), 0.0), axis=1, keepdims=True)
    w_nine = jnp.sum(jnp.where(ninth, wt, 0.0), axis=1, keepdims=True)
    weight = jnp.concatenate([w_main, w_nine], axis=0)
    u_low = nt(g[...], dsec[...])
    cot_low = (weight * u_low).astype(bf16)
    sg0 = SCALE * jnp.sum(hidden_low.astype(f32) * u_low, axis=1, keepdims=True)
    bgl = jnp.zeros((ROWS, 16), f32)
    bul = jnp.zeros((ROWS, 16), f32)

    def backward(n, carry):
        slot_gate, bg, bu = carry
        c = lanes(n)
        y_done(6 + n)
        u = nn(g[...], wbuf[6 + n])
        slot_gate = slot_gate + jnp.sum(hid[:, c].astype(f32) * u, axis=1, keepdims=True)
        hg = weight * u + SCALE * nn(cot_low, dfT[:, c])
        gg = (hg * coef[:, c]).astype(bf16)
        ug = (hg * act[:, c]).astype(bf16)
        ggp[:, c] = gg
        ugp[:, c] = ug
        return slot_gate, bg + nt(gg, gs[:, c]), bu + nt(ug, us[:, c])

    slot_gate, bgl, bul = lax.fori_loop(0, F // 256, backward, (sg0, bgl, bul))
    bgl = bgl.astype(bf16)
    bul = bul.astype(bf16)

    bl = jnp.concatenate([bgl, bul], axis=1)

    def store4(first, value):
        for j in range(4):
            ad_send[first + j] = value[:, j * 640 : (j + 1) * 640]

    ins = (SCALE * tn(bl, x[...])).astype(bf16)
    store4(0, ins[0:16])
    store4(4, ins[16:32])
    whl = (weight * hidden_low.astype(f32)).astype(bf16)
    store4(8, (SCALE * tn(whl, g[...])).astype(bf16))
    store4(12, jnp.concatenate([
        (SCALE * tn(gate_low, ggp[...])).astype(bf16),
        (SCALE * tn(up_low, ugp[...])).astype(bf16),
        (SCALE * tn(cot_low, hid[...])).astype(bf16),
        jnp.zeros((16, 256), bf16),
    ], axis=1))

    def part_copy(phase, there, here):
        if phase == 0:
            src, dst = ad_send.at[there], ad_recv.at[here]
        else:
            src, dst = ad_one, ad_all.at[here]
        return pltpu.make_async_remote_copy(
            src_ref=src,
            dst_ref=dst,
            send_sem=a_send.at[phase, there],
            recv_sem=a_recv.at[phase, here],
            device_id={"dp": there},
            device_id_type=MESH,
        )

    def part_wait(phase):
        def body(k):
            p = dp_peer(k)
            part_copy(phase, p, p).wait()

        loop(ND - 1, body)

    loop(ND - 1, lambda k: part_copy(0, dp_peer(k), dp).start())
    ad_recv[dp] = ad_send[dp]

    def slot_grad(n):
        c = pl.ds(pl.multiple_of(n * 256, 256), 256)
        value = SCALE * (nn(bgl, gfT[:, c]) + nn(bul, ufT[:, c]))
        for k in range(3):
            f = slice(k * 256, (k + 1) * 256)
            value = value + nt(ggp[:, f], wbuf[2 * k, c, :])
            value = value + nt(ugp[:, f], wbuf[2 * k + 1, c, :])
        sg[:, c] = value.astype(bf16)

    loop(D // 256, slot_grad)

    part_wait(0)

    def both(j, t):
        return t[0] + ad_recv[2 * j].astype(f32), t[1] + ad_recv[2 * j + 1].astype(f32)

    zero = jnp.zeros((16, 640), f32)
    here, there = lax.fori_loop(0, ND // 2, both, (zero, zero))
    ad_far[...] = there
    far = pltpu.make_async_remote_copy(
        src_ref=ad_far, dst_ref=ad_near, send_sem=f_send.at[0], recv_sem=f_recv.at[0],
        device_id={"expert": z_from * 2 + c}, device_id_type=MESH,
    )
    far.start()

    def pack(n):
        both = jnp.concatenate([sg[0:256, lanes(n)], sg[0:256, lanes(n, start=H)]], axis=0)
        send[2, :, lanes(n)] = nn(fold[...], both).astype(bf16)

    loop(H // 256, pack)
    back = nn(gather, jnp.where(diag, slot_gate[0:256], 0.0).astype(bf16))
    back = back + jnp.where(ninth, slot_gate[256:ROWS], 0.0)
    tail_to_block(2, sg[256:ROWS, :], back.astype(bf16))
    rows_back()

    far.wait()
    total = (here + ad_near[...]).astype(bf16)
    ad_one[...] = total
    loop(ND - 1, lambda k: part_copy(1, dp_peer(k), dp).start())
    ad_all[dp] = total
    part_wait(1)

    ggi[...] = load4(ad_all, 0).astype(f32)
    gui[...] = load4(ad_all, 4).astype(f32)
    gdo[...] = load4(ad_all, 8).astype(f32)
    rest = load4(ad_all, 12).astype(f32)
    ggo[...] = rest[:, 0:F]
    guo[...] = rest[:, F : 2 * F]
    gdi[...] = rest[:, 2 * F : 3 * F]


    def all_sent(t):
        move(t).wait_send()
        x_sent(t)
        for way in range(2):
            along_y(t, way, 1).wait_send()
            along_y(t, way, 2).wait_send()

    all_sent(AD)
    loop(PIECES, all_sent)
    rows_sent(0, mine)
    rows_sent(1, mine)
    rows_sent(2, my_slot)
    rows_wait(2, mine)
    nine = jnp.concatenate(tail_from_block(2), axis=1)
    sg[0:NE, :] = nine

    def combine(n):
        r = recv[2, :, lanes(n)]
        left = tn(sel[:, 0:TD], r) + tn(sel9, sg[0:NE, lanes(n)])
        right = tn(sel[:, TD : 2 * TD], r) + tn(sel9, sg[0:NE, lanes(n, start=H)])
        tg_out[:, lanes(n)] = left.astype(bf16)
        tg_out[:, lanes(n, start=H)] = right.astype(bf16)

    loop(H // 256, combine)
    wt3 = nn(take_weight, recv[2, :, H + 128 : BW]).astype(bf16)
    for k in range(2):
        picked = tn(wt3, hot[k].astype(bf16))
        gg_out[k : k + 1, :] = jnp.sum(
            jnp.where(r128 == slots[k], picked, 0.0), axis=0, keepdims=True
        )


def per_device(tokens, out_grad, expert_ids, gate_values, wg, wu, wd, gf, gs, uf, us, df, ds):
    vmem = pl.BlockSpec(memory_space=pltpu.VMEM)
    anywhere = pl.BlockSpec(memory_space=pl.ANY)
    shape = jax.ShapeDtypeStruct
    outs = pl.pallas_call(
        kernel,
        out_shape=(
            shape((TD, D), bf16),
            shape((2, TD), f32),
            shape((16, D), f32),
            shape((16, F), f32),
            shape((16, D), f32),
            shape((16, F), f32),
            shape((16, F), f32),
            shape((16, D), f32),
        ),
        in_specs=[vmem] * 4 + [anywhere] * 3 + [vmem] * 6,
        out_specs=[vmem] * 8,
        scratch_shapes=[
            pltpu.VMEM((3, 512, BW), bf16),
            pltpu.VMEM((3, 512, BW), bf16),
            pltpu.VMEM((PIECES, D, 256), bf16),
            pltpu.VMEM((512, 2 * TD), bf16),
            pltpu.VMEM((512, 512), bf16),
            pltpu.VMEM((512, 512), bf16),
            pltpu.VMEM((512, 512), bf16),
            pltpu.VMEM((512, 512), bf16),
            pltpu.VMEM((ROWS, D), bf16),
            pltpu.VMEM((ROWS, D), bf16),
            pltpu.VMEM((ROWS, D), bf16),
            pltpu.VMEM((ROWS, F), f32),
            pltpu.VMEM((ROWS, F), f32),
            pltpu.VMEM((ROWS, F), bf16),
            pltpu.VMEM((ROWS, F), bf16),
            pltpu.VMEM((ROWS, F), bf16),
            pltpu.VMEM((16, 16, 640), bf16),
            pltpu.VMEM((16, 16, 640), bf16),
            pltpu.VMEM((16, 640), bf16),
            pltpu.VMEM((16, 16, 640), bf16),
            pltpu.VMEM((16, 640), f32),
            pltpu.VMEM((16, 640), f32),
            pltpu.VMEM((16, D), bf16),
            pltpu.VMEM((16, D), bf16),
            pltpu.VMEM((16, D), bf16),
            pltpu.VMEM((16, F), bf16),
            pltpu.VMEM((16, F), bf16),
            pltpu.VMEM((16, F), bf16),
            pltpu.VMEM((PIECES, SH, 256), bf16),
            pltpu.VMEM((PIECES, SH, 256), bf16),
            pltpu.VMEM((16, 16, 640), bf16),
            pltpu.VMEM((16, 640), bf16),
            pltpu.VMEM((16, 16, 640), bf16),
            pltpu.SemaphoreType.DMA((3, NE)),
            pltpu.SemaphoreType.DMA((3, NE)),
            pltpu.SemaphoreType.DMA((PIECES,)),
            pltpu.SemaphoreType.DMA((PIECES + 1,)),
            pltpu.SemaphoreType.DMA((PIECES + 1,)),
            pltpu.SemaphoreType.DMA((PIECES + 1, 4)),
            pltpu.SemaphoreType.DMA((PIECES + 1, 4)),
            pltpu.SemaphoreType.DMA((PIECES + 1,)),
            pltpu.SemaphoreType.DMA((PIECES + 1, 2)),
            pltpu.SemaphoreType.DMA((PIECES + 1, 2)),
            pltpu.SemaphoreType.DMA((PIECES + 1, 2)),
            pltpu.SemaphoreType.DMA((PIECES + 1, 2)),
            pltpu.SemaphoreType.DMA((2, ND)),
            pltpu.SemaphoreType.DMA((2, ND)),
            pltpu.SemaphoreType.DMA((1,)),
            pltpu.SemaphoreType.DMA((1,)),
        ],
        compiler_params=pltpu.CompilerParams(
            collective_id=0, has_side_effects=True, vmem_limit_bytes=58 * 2**20
        ),
        cost_estimate=pl.CostEstimate(
            flops=8_000_000_000, bytes_accessed=20_000_000, transcendentals=300_000
        ),
    )(
        tokens, out_grad, expert_ids.T, gate_values.T, wg[0], wu[0], wd[0],
        gf[0].T, gs[0], uf[0].T, us[0], df[0].T, ds[0],
    )
    tg, gg, ggi, ggo, gui, guo, gdi, gdo = outs
    return tg, gg.T, ggi.T[None], ggo[None], gui.T[None], guo[None], gdi.T[None], gdo[None]


def solution(mesh):
    row = P(("dp", "expert"), None)
    frozen = P("expert", "dp", None)
    one = P("expert", None, None)
    return jax.shard_map(
        per_device,
        mesh=mesh,
        in_specs=(row,) * 4 + (frozen,) * 3 + (one,) * 6,
        out_specs=(row,) * 2 + (one,) * 6,
        check_vma=False,
    )
```

```python
import functools

import jax
import jax.numpy as jnp
from jax import lax
from jax.experimental import pallas as pl
from jax.experimental.pallas import tpu as pltpu
from jax.sharding import PartitionSpec as P

MESH = pl.DeviceIdType.MESH
bf16 = jnp.bfloat16
f32 = jnp.float32
i32 = jnp.int32

NE, ND = 32, 16
TD, D, F = 128, 2560, 768
H = D // 2
SH = D // ND
ROWS = 288
BW = H + 256
PIECES = 9
SCALE = 2.0


def nn(a, b):
    return lax.dot_general(a, b, (((1,), (0,)), ((), ())), preferred_element_type=f32)


def nt(a, b):
    return lax.dot_general(a, b, (((1,), (1,)), ((), ())), preferred_element_type=f32)


def tn(a, b):
    return lax.dot_general(a, b, (((0,), (0,)), ((), ())), preferred_element_type=f32)


def iota(shape, axis):
    return lax.broadcasted_iota(i32, shape, axis)


def flag(mask):
    return jnp.where(mask, 1.0, 0.0).astype(bf16)


def loop(n, body):
    def step(k, carry):
        body(k)
        return carry

    lax.fori_loop(0, n, step, 0)


def lanes(n, width=256, start=0):
    return pl.ds(pl.multiple_of(n * width + start, 128), width)


def pair_slots(ids):
    e32 = iota((NE, TD), 0)
    id0, id1 = ids[0:1, :], ids[1:2, :]
    hot = [jnp.where(e32 == id0, 1.0, 0.0), jnp.where(e32 == id1, 1.0, 0.0)]
    earlier = flag(iota((TD, TD), 0) < iota((TD, TD), 1))
    before = nn((hot[0] + hot[1]).astype(bf16), earlier)
    slots = [jnp.sum(before * h, axis=0, keepdims=True).astype(i32) for h in hot]
    sel9 = (
        jnp.where(slots[0] == 8, hot[0], 0.0) + jnp.where(slots[1] == 8, hot[1], 0.0)
    ).astype(bf16)
    return id0, id1, hot, slots, sel9


def kernel(
    tok, grd, ids, gates, wg, wu, wd, in_gf, in_gs, in_uf, in_us, in_df, in_ds,
    block_out, sel_out, perm_out, ad_out,
    send, recv, wbuf, sel, perm, permT, fold, unfold, x, g, sg, coef, act, hid, ggp, ugp,
    ad_send, ad_recv, ad_one, ad_all, ad_far, ad_near,
    gfT, ufT, dsec, gs, us, dfT, staged, moved, packed, ad_moved, ad_buf,
    s_send, s_recv, st_sem, m_send, m_recv, x_send, x_recv, x_own,
    y1_send, y1_recv, y2_send, y2_recv, a_send, a_recv, f_send, f_recv, o_sem,
):
    me = lax.axis_index("expert")
    dp = lax.axis_index("dp")

    z, c = me // 2, me % 2
    y, xx = dp // 4, dp % 4
    b = dp % 2
    odd = (b + c) % 2

    mine = ((z + 16 + b * (14 * c - 7)) % 16) * 2 + c
    my_slot = b * 16 + (3 + odd) * 2 + c
    my_k = c + 2 * b + 4 * (3 + odd)
    z_to = (z + 23 - 14 * c) % 16
    z_from = (z + 9 + 14 * c) % 16

    def home(k):
        c2, b2, j = k % 2, (k // 2) % 2, k // 4
        zp = (z + 13 + j - (b2 + c2) % 2) % 16
        expert = ((zp + 16 + b2 * (14 * c2 - 7)) % 16) * 2 + c2
        return dp - b + b2, zp * 2 + c2, expert, b * 16 + j * 2 + c

    def origin(slot):
        cs, j, bs = slot % 2, (slot % 16) // 2, slot // 16
        zs = (z + 19 - j + odd) % 16
        return dp - b + bs, zs * 2 + cs

    def dp_peer(k):
        return (dp + 1 + k) % ND

    bar = pltpu.get_barrier_semaphore()

    def greet(d, e):
        pl.semaphore_signal(
            bar, inc=1, device_id={"dp": d, "expert": e}, device_id_type=MESH)

    def greet_rows(k):
        i = (2 * b + c + 16 + 1 + k) % 36
        greet(dp - b + (i // 2) % 2, ((z + 12 + i // 4) % 16) * 2 + i % 2)

    loop(35, greet_rows)
    greet(dp, z_to * 2 + c)
    greet(dp, z_from * 2 + c)
    loop(ND - 1, lambda k: greet(dp_peer(k), me))

    def block(p):
        return pl.ds(pl.multiple_of(p * 16, 16), 16)

    def row_copy(buf, src, dst, d, e):
        return pltpu.make_async_remote_copy(
            src_ref=send.at[buf, block(src)],
            dst_ref=recv.at[buf, block(dst)],
            send_sem=s_send.at[buf, src],
            recv_sem=s_recv.at[buf, dst],
            device_id={"dp": d, "expert": e},
            device_id_type=MESH,
        )

    def rows_start(buf):
        def body(i):
            d, e, expert, slot = home((my_k + 1 + i) % NE)
            row_copy(buf, expert, slot, d, e).start()

        loop(NE - 1, body)
        recv[buf, block(my_slot), :] = send[buf, block(mine), :]

    CUT = 512

    def back_copy(part, src, dst, d, e):
        c = pl.ds(0, CUT) if part == 0 else pl.ds(CUT, BW - CUT)
        return pltpu.make_async_remote_copy(
            src_ref=send.at[2, block(src), c],
            dst_ref=recv.at[2, block(dst), c],
            send_sem=s_send.at[2 + part, src],
            recv_sem=s_recv.at[2 + part, dst],
            device_id={"dp": d, "expert": e},
            device_id_type=MESH,
        )

    def rows_back(part):
        def body(i):
            slot = (my_slot + 1 + i) % NE
            d, e = origin(slot)
            back_copy(part, slot, mine, d, e).start()

        loop(NE - 1, body)
        c = slice(0, CUT) if part == 0 else slice(CUT, BW)
        recv[2, block(mine), c] = send[2, block(my_slot), c]

    def back_wait(part):
        loop(NE - 1, lambda i: back_copy(
            part, (mine + 1 + i) % NE, (mine + 1 + i) % NE, dp, z_to * 2 + c).wait_recv())

    def back_sent(part):
        loop(NE - 1, lambda i: back_copy(
            part, (my_slot + 1 + i) % NE, (my_slot + 1 + i) % NE, dp, z_to * 2 + c).wait_send())

    def rows_wait(buf, own):
        loop(NE - 1, lambda i: row_copy(
            buf, (own + 1 + i) % NE, (own + 1 + i) % NE, dp, z_to * 2 + c).wait_recv())

    def rows_sent(buf, own):
        loop(NE - 1, lambda i: row_copy(
            buf, (own + 1 + i) % NE, (own + 1 + i) % NE, dp, z_to * 2 + c).wait_send())

    AD = PIECES

    def stage(t):
        ref, n = ((wg, wu)[t % 2], t // 2) if t < 6 else (wd, t - 6)
        return pltpu.make_async_copy(
            ref.at[:, n * 256 : (n + 1) * 256], staged.at[t], st_sem.at[t])

    for t in range(PIECES):
        stage(t).start()

    def is_ad(t):
        return isinstance(t, int) and t == AD

    def first_of(t):
        return packed.at[dp] if is_ad(t) else staged.at[t]

    def second_of(t):
        return ad_moved if is_ad(t) else moved.at[t]

    def shard(t, d):
        if is_ad(t):
            return ad_buf.at[d]
        return wbuf.at[t, pl.ds(pl.multiple_of(d * SH, 32), SH)]

    def four(t, row, part):
        if is_ad(t):
            return ad_buf.at[pl.ds(row * 4 + (2 if part == 2 else 0), 2 if part else 4)]
        first = row * 4 * SH + (2 * SH if part == 2 else 0)
        return wbuf.at[t, pl.ds(pl.multiple_of(first, 64), (2 if part else 4) * SH)]

    def move(t):
        return pltpu.make_async_remote_copy(
            src_ref=first_of(t), dst_ref=second_of(t), send_sem=m_send.at[t], recv_sem=m_recv.at[t],
            device_id={"expert": z_to * 2 + c}, device_id_type=MESH,
        )

    def along_x(t, src, to, at):
        return pltpu.make_async_remote_copy(
            src_ref=src, dst_ref=shard(t, y * 4 + at),
            send_sem=x_send.at[t, to], recv_sem=x_recv.at[t, at],
            device_id={"dp": y * 4 + to}, device_id_type=MESH,
        )

    def x_start(t, stream):
        src = first_of(t) if stream == 0 else second_of(t)

        def body(i):
            to = stream + 2 * i

            @pl.when(to != xx)
            def _():
                along_x(t, src, to, xx).start()

            @pl.when(to == xx)
            def _():
                pltpu.make_async_copy(src, shard(t, dp), x_own.at[t]).start()

        loop(2, body)

    def x_wait(t):
        loop(3, lambda i: along_x(
            t, first_of(t), (xx + 1 + i) % 4, (xx + 1 + i) % 4).wait_recv())
        pltpu.make_async_copy(first_of(t), shard(t, dp), x_own.at[t]).wait()

    def x_sent(t):
        loop(3, lambda i: along_x(
            t, first_of(t), (xx + 1 + i) % 4, (xx + 1 + i) % 4).wait_send())

    ends = ((y + 1) % 4, (y + 3) % 4)

    def along_y(t, way, hop):
        region = four(t, y, 0) if hop == 1 else four(t, ends[1 - way], way + 1)
        sems = (y1_send, y1_recv) if hop == 1 else (y2_send, y2_recv)
        return pltpu.make_async_remote_copy(
            src_ref=region, dst_ref=region,
            send_sem=sems[0].at[t, way], recv_sem=sems[1].at[t, way],
            device_id={"dp": ends[way] * 4 + xx}, device_id_type=MESH,
        )

    def landed_y(t, way, hop):
        region = four(t, ends[1 - way], 0) if hop == 1 else four(t, (y + 2) % 4, way + 1)
        sems = (y1_send, y1_recv) if hop == 1 else (y2_send, y2_recv)
        pltpu.make_async_remote_copy(
            src_ref=region, dst_ref=region,
            send_sem=sems[0].at[t, way], recv_sem=sems[1].at[t, way],
            device_id={"dp": ends[way] * 4 + xx}, device_id_type=MESH,
        ).wait_recv()

    def move_done(t):
        move(t).wait_recv()
        x_start(t, 1)

    def y_first(t):
        x_wait(t)
        along_y(t, 0, 1).start()
        along_y(t, 1, 1).start()

    def y_second(t):
        for way in range(2):
            landed_y(t, way, 1)
            along_y(t, way, 2).start()

    def y_done(t):
        landed_y(t, 0, 2)
        landed_y(t, 1, 2)

    for first, ref in ((0, in_gf), (4, in_uf), (8, in_ds)):
        for j in range(4):
            packed[first + j] = ref[:, j * 640 : (j + 1) * 640]
    small = jnp.concatenate(
        [in_gs[...], in_us[...], in_df[...], jnp.zeros((16, 256), bf16)], axis=1
    )
    for j in range(4):
        packed[12 + j] = small[:, j * 640 : (j + 1) * 640]

    for t in range(PIECES):
        stage(t).wait()
    pl.semaphore_wait(bar, 35 + 2 + ND - 1)
    move(AD).start()
    loop(PIECES, lambda t: move(t).start())
    x_start(AD, 0)
    loop(PIECES, lambda t: x_start(t, 0))

    id0, id1, hot, slots, sel9 = pair_slots(ids)
    q512 = iota((512, TD), 0)
    keys = [
        jnp.where(slots[0] < 8, id0 * 16 + slots[0], -16),
        jnp.where(slots[1] < 8, id1 * 16 + slots[1], -16),
    ]
    sel[:, 0:TD] = flag((q512 == keys[0]) | (q512 == keys[1]))
    sel[:, TD : 2 * TD] = flag((q512 == keys[0] + 8) | (q512 == keys[1] + 8))
    qa, qb = iota((512, 512), 0), iota((512, 512), 1)
    perm[...] = flag(qb == (qa % 16) * 32 + qa // 16)
    permT[...] = flag(qa == (qb % 16) * 32 + qb // 16)
    cb = qb % 256
    fold[...] = flag(qa == (cb // 8) * 16 + cb % 8 + (qb // 256) * 8)
    ca = qa % 256
    unfold[...] = flag(qb == (ca // 8) * 16 + ca % 8 + (qa // 256) * 8)
    put_weight = flag(iota((512, NE), 0) == iota((512, NE), 1) * 16 + 4)
    take_weight = flag(iota((NE, 512), 1) == iota((NE, 512), 0) * 16 + 4)


    def tail_to_block(buf, nine, extra):
        first = jnp.concatenate([nine[:, j * 128 : (j + 1) * 128] for j in range(16)], axis=0)
        last = jnp.concatenate([nine[:, j * 128 : (j + 1) * 128] for j in range(16, 20)], axis=0)
        send[buf, :, H : H + 128] = nn(perm[...], first).astype(bf16)
        z1 = nn(perm[:, 0:128], last)
        if extra is not None:
            z1 = z1 + nn(put_weight, extra)
        send[buf, :, H + 128 : BW] = z1.astype(bf16)

    def tail_from_block(buf):
        first = nn(permT[...], recv[buf, :, H : H + 128]).astype(bf16)
        last = nn(permT[0:128, :], recv[buf, :, H + 128 : BW]).astype(bf16)
        parts = [first[j * 32 : (j + 1) * 32] for j in range(16)]
        parts += [last[j * 32 : (j + 1) * 32] for j in range(4)]
        return parts

    def dispatch(buf, src, extra):
        def body(n):
            both = jnp.concatenate([src[:, lanes(n)], src[:, lanes(n, start=H)]], axis=0)
            send[buf, :, lanes(n)] = nn(sel[...], both).astype(bf16)

        loop(H // 256, body)
        tail_to_block(buf, nn(sel9, src[...]).astype(bf16), extra)

    dispatch(0, tok, None)
    rows_start(0)
    sel_copy = pltpu.make_async_copy(sel, sel_out, o_sem.at[0])
    sel_copy.start()
    perm_copy = pltpu.make_async_copy(permT, perm_out, o_sem.at[1])
    perm_copy.start()
    r128 = iota((128, TD), 0)
    weights = 0.0
    for k in range(2):
        a = (hot[k] * gates[k : k + 1, :]).astype(bf16)
        weights = weights + nt(a, flag(r128 == slots[k]))
    dispatch(1, grd, weights.astype(bf16))
    rows_start(1)

    move_done(AD)
    move_done(0)
    y_first(AD)
    move_done(1)
    y_first(0)
    y_second(AD)

    def relay(i):
        move_done(i + 2)
        y_first(i + 1)
        y_second(i)

    loop(PIECES - 2, relay)
    y_first(PIECES - 1)

    def receive(buf, dst):
        def body(n):
            both = nn(unfold[...], recv[buf, :, lanes(n)]).astype(bf16)
            dst[0:256, lanes(n)] = both[0:256]
            dst[0:256, lanes(n, start=H)] = both[256:512]

        loop(H // 256, body)
        for j, part in enumerate(tail_from_block(buf)):
            dst[256:ROWS, j * 128 : (j + 1) * 128] = part

    rows_wait(0, my_slot)
    receive(0, x)
    y_done(AD)

    def load4(buf, first):
        return jnp.concatenate([buf[first + j] for j in range(4)], axis=1)

    gfT[...] = load4(ad_buf, 0)
    ufT[...] = load4(ad_buf, 4)
    dsec[...] = load4(ad_buf, 8)
    rest = load4(ad_buf, 12)
    gs[...] = rest[:, 0:F]
    us[...] = rest[:, F : 2 * F]
    dfT[...] = rest[:, 2 * F : 3 * F]
    low = nt(x[...], jnp.concatenate([gfT[...], ufT[...]], axis=0)).astype(bf16)
    gate_low, up_low = low[:, 0:16], low[:, 16:32]
    y_second(PIECES - 2)
    y_second(PIECES - 1)

    def forward(n):
        c = lanes(n)
        y_done(2 * n)
        pre = nn(x[...], wbuf[2 * n]) + SCALE * nn(gate_low, gs[:, c])
        y_done(2 * n + 1)
        up = nn(x[...], wbuf[2 * n + 1]) + SCALE * nn(up_low, us[:, c])
        s = jax.nn.sigmoid(pre)
        a = pre * s
        act[:, c] = a
        coef[:, c] = up * s * (1.0 + pre * (1.0 - s))
        hid[:, c] = (a * up).astype(bf16)

    loop(F // 256, forward)
    hidden_low = nt(hid[...], dfT[...]).astype(bf16)

    rows_wait(1, my_slot)
    receive(1, g)
    wt = nn(take_weight, recv[1, :, H + 128 : BW])
    p256 = iota((256, 128), 0)
    l256 = iota((256, 128), 1)
    spread = flag(iota((256, NE), 0) // 8 == iota((256, NE), 1))
    gather = flag(iota((NE, 256), 1) // 8 == iota((NE, 256), 0))
    diag = l256 == p256 % 8
    ninth = iota((NE, 128), 1) == 8
    w_main = jnp.sum(jnp.where(diag, nn(spread, wt.astype(bf16)), 0.0), axis=1, keepdims=True)
    w_nine = jnp.sum(jnp.where(ninth, wt, 0.0), axis=1, keepdims=True)
    weight = jnp.concatenate([w_main, w_nine], axis=0)
    u_low = nt(g[...], dsec[...])
    cot_low = (weight * u_low).astype(bf16)
    sg0 = SCALE * jnp.sum(hidden_low.astype(f32) * u_low, axis=1, keepdims=True)
    bgl = jnp.zeros((ROWS, 16), f32)
    bul = jnp.zeros((ROWS, 16), f32)

    def backward(n, carry):
        slot_gate, bg, bu = carry
        c = lanes(n)
        y_done(6 + n)
        u = nn(g[...], wbuf[6 + n])
        slot_gate = slot_gate + jnp.sum(hid[:, c].astype(f32) * u, axis=1, keepdims=True)
        hg = weight * u + SCALE * nn(cot_low, dfT[:, c])
        gg = (hg * coef[:, c]).astype(bf16)
        ug = (hg * act[:, c]).astype(bf16)
        ggp[:, c] = gg
        ugp[:, c] = ug
        return slot_gate, bg + nt(gg, gs[:, c]), bu + nt(ug, us[:, c])

    slot_gate, bgl, bul = lax.fori_loop(0, F // 256, backward, (sg0, bgl, bul))
    bgl = bgl.astype(bf16)
    bul = bul.astype(bf16)

    def slot_grad(n):
        c = pl.ds(pl.multiple_of(n * 256, 256), 256)
        value = SCALE * (nn(bgl, gfT[:, c]) + nn(bul, ufT[:, c]))
        for k in range(3):
            f = slice(k * 256, (k + 1) * 256)
            value = value + nt(ggp[:, f], wbuf[2 * k, c, :])
            value = value + nt(ugp[:, f], wbuf[2 * k + 1, c, :])
        sg[:, c] = value.astype(bf16)

    def pack(n):
        both = jnp.concatenate([sg[0:256, lanes(n)], sg[0:256, lanes(n, start=H)]], axis=0)
        send[2, :, lanes(n)] = nn(fold[...], both).astype(bf16)

    def both_halves(n):
        slot_grad(n)
        slot_grad(n + H // 256)
        pack(n)

    loop(CUT // 256, both_halves)
    rows_back(0)

    bl = jnp.concatenate([bgl, bul], axis=1)

    def store4(first, value):
        for j in range(4):
            ad_send[first + j] = value[:, j * 640 : (j + 1) * 640]

    ins = (SCALE * tn(bl, x[...])).astype(bf16)
    store4(0, ins[0:16])
    store4(4, ins[16:32])
    whl = (weight * hidden_low.astype(f32)).astype(bf16)
    store4(8, (SCALE * tn(whl, g[...])).astype(bf16))
    store4(12, jnp.concatenate([
        (SCALE * tn(gate_low, ggp[...])).astype(bf16),
        (SCALE * tn(up_low, ugp[...])).astype(bf16),
        (SCALE * tn(cot_low, hid[...])).astype(bf16),
        jnp.zeros((16, 256), bf16),
    ], axis=1))

    def part_copy(phase, there, here):
        if phase == 0:
            src, dst = ad_send.at[there], ad_recv.at[here]
        else:
            src, dst = ad_one, ad_all.at[here]
        return pltpu.make_async_remote_copy(
            src_ref=src,
            dst_ref=dst,
            send_sem=a_send.at[phase, there],
            recv_sem=a_recv.at[phase, here],
            device_id={"dp": there},
            device_id_type=MESH,
        )

    def part_wait(phase):
        def body(k):
            p = dp_peer(k)
            part_copy(phase, p, p).wait()

        loop(ND - 1, body)

    loop(ND - 1, lambda k: part_copy(0, dp_peer(k), dp).start())
    ad_recv[dp] = ad_send[dp]

    loop(H // 256 - CUT // 256, lambda n: both_halves(n + CUT // 256))
    back = nn(gather, jnp.where(diag, slot_gate[0:256], 0.0).astype(bf16))
    back = back + jnp.where(ninth, slot_gate[256:ROWS], 0.0)
    tail_to_block(2, sg[256:ROWS, :], back.astype(bf16))
    part_wait(0)

    def both(j, t):
        return t[0] + ad_recv[2 * j].astype(f32), t[1] + ad_recv[2 * j + 1].astype(f32)

    zero = jnp.zeros((16, 640), f32)
    here, there = lax.fori_loop(0, ND // 2, both, (zero, zero))
    ad_far[...] = there
    far = pltpu.make_async_remote_copy(
        src_ref=ad_far, dst_ref=ad_near, send_sem=f_send.at[0], recv_sem=f_recv.at[0],
        device_id={"expert": z_from * 2 + c}, device_id_type=MESH,
    )
    far.start()
    rows_back(1)

    far.wait()
    total = (here + ad_near[...]).astype(bf16)
    ad_one[...] = total
    loop(ND - 1, lambda k: part_copy(1, dp_peer(k), dp).start())
    ad_all[dp] = total
    part_wait(1)

    ad_copy = pltpu.make_async_copy(ad_all, ad_out, o_sem.at[2])
    ad_copy.start()

    def all_sent(t):
        move(t).wait_send()
        x_sent(t)
        for way in range(2):
            along_y(t, way, 1).wait_send()
            along_y(t, way, 2).wait_send()

    all_sent(AD)
    loop(PIECES, all_sent)
    rows_sent(0, mine)
    rows_sent(1, mine)
    back_sent(0)
    back_sent(1)
    back_wait(0)
    back_wait(1)
    block_copy = pltpu.make_async_copy(recv.at[2], block_out, o_sem.at[3])
    block_copy.start()
    for copy in (sel_copy, perm_copy, ad_copy, block_copy):
        copy.wait()


def combine_kernel(
    blocks, sel, permT, sums, ids, tg_out, gg_out, ggi, ggo, gui, guo, gdi, gdo, sg
):
    _, _, hot, slots, sel9 = pair_slots(ids)
    first = nn(permT[...], blocks[:, H : H + 128]).astype(bf16)
    last = nn(permT[0:128, :], blocks[:, H + 128 : BW]).astype(bf16)
    for j in range(16):
        sg[:, j * 128 : (j + 1) * 128] = first[j * 32 : (j + 1) * 32]
    for j in range(4):
        sg[:, (16 + j) * 128 : (17 + j) * 128] = last[j * 32 : (j + 1) * 32]

    def combine(n):
        r = blocks[:, lanes(n)]
        left = tn(sel[:, 0:TD], r) + tn(sel9, sg[:, lanes(n)])
        right = tn(sel[:, TD : 2 * TD], r) + tn(sel9, sg[:, lanes(n, start=H)])
        tg_out[:, lanes(n)] = left.astype(bf16)
        tg_out[:, lanes(n, start=H)] = right.astype(bf16)

    loop(H // 256, combine)
    take_weight = flag(iota((NE, 512), 1) == iota((NE, 512), 0) * 16 + 4)
    r128 = iota((128, TD), 0)
    wt3 = nn(take_weight, blocks[:, H + 128 : BW]).astype(bf16)
    for k in range(2):
        picked = tn(wt3, hot[k].astype(bf16))
        gg_out[k : k + 1, :] = jnp.sum(
            jnp.where(r128 == slots[k], picked, 0.0), axis=0, keepdims=True
        )

    def load4(first):
        return jnp.concatenate([sums[first + j] for j in range(4)], axis=1).astype(f32)

    ggi[...] = load4(0)
    gui[...] = load4(4)
    gdo[...] = load4(8)
    rest = load4(12)
    ggo[...] = rest[:, 0:F]
    guo[...] = rest[:, F : 2 * F]
    gdi[...] = rest[:, 2 * F : 3 * F]


def per_device(tokens, out_grad, expert_ids, gate_values, wg, wu, wd, gf, gs, uf, us, df, ds):
    vmem = pl.BlockSpec(memory_space=pltpu.VMEM)
    anywhere = pl.BlockSpec(memory_space=pl.ANY)
    shape = jax.ShapeDtypeStruct
    blocks, sel, permT, sums = pl.pallas_call(
        kernel,
        out_shape=(
            shape((512, BW), bf16),
            shape((512, 2 * TD), bf16),
            shape((512, 512), bf16),
            shape((16, 16, 640), bf16),
        ),
        in_specs=[vmem] * 4 + [anywhere] * 3 + [vmem] * 6,
        out_specs=[anywhere] * 4,
        scratch_shapes=[
            pltpu.VMEM((3, 512, BW), bf16),
            pltpu.VMEM((3, 512, BW), bf16),
            pltpu.VMEM((PIECES, D, 256), bf16),
            pltpu.VMEM((512, 2 * TD), bf16),
            pltpu.VMEM((512, 512), bf16),
            pltpu.VMEM((512, 512), bf16),
            pltpu.VMEM((512, 512), bf16),
            pltpu.VMEM((512, 512), bf16),
            pltpu.VMEM((ROWS, D), bf16),
            pltpu.VMEM((ROWS, D), bf16),
            pltpu.VMEM((ROWS, D), bf16),
            pltpu.VMEM((ROWS, F), f32),
            pltpu.VMEM((ROWS, F), f32),
            pltpu.VMEM((ROWS, F), bf16),
            pltpu.VMEM((ROWS, F), bf16),
            pltpu.VMEM((ROWS, F), bf16),
            pltpu.VMEM((16, 16, 640), bf16),
            pltpu.VMEM((16, 16, 640), bf16),
            pltpu.VMEM((16, 640), bf16),
            pltpu.VMEM((16, 16, 640), bf16),
            pltpu.VMEM((16, 640), f32),
            pltpu.VMEM((16, 640), f32),
            pltpu.VMEM((16, D), bf16),
            pltpu.VMEM((16, D), bf16),
            pltpu.VMEM((16, D), bf16),
            pltpu.VMEM((16, F), bf16),
            pltpu.VMEM((16, F), bf16),
            pltpu.VMEM((16, F), bf16),
            pltpu.VMEM((PIECES, SH, 256), bf16),
            pltpu.VMEM((PIECES, SH, 256), bf16),
            pltpu.VMEM((16, 16, 640), bf16),
            pltpu.VMEM((16, 640), bf16),
            pltpu.VMEM((16, 16, 640), bf16),
            pltpu.SemaphoreType.DMA((4, NE)),
            pltpu.SemaphoreType.DMA((4, NE)),
            pltpu.SemaphoreType.DMA((PIECES,)),
            pltpu.SemaphoreType.DMA((PIECES + 1,)),
            pltpu.SemaphoreType.DMA((PIECES + 1,)),
            pltpu.SemaphoreType.DMA((PIECES + 1, 4)),
            pltpu.SemaphoreType.DMA((PIECES + 1, 4)),
            pltpu.SemaphoreType.DMA((PIECES + 1,)),
            pltpu.SemaphoreType.DMA((PIECES + 1, 2)),
            pltpu.SemaphoreType.DMA((PIECES + 1, 2)),
            pltpu.SemaphoreType.DMA((PIECES + 1, 2)),
            pltpu.SemaphoreType.DMA((PIECES + 1, 2)),
            pltpu.SemaphoreType.DMA((2, ND)),
            pltpu.SemaphoreType.DMA((2, ND)),
            pltpu.SemaphoreType.DMA((1,)),
            pltpu.SemaphoreType.DMA((1,)),
            pltpu.SemaphoreType.DMA((4,)),
        ],
        compiler_params=pltpu.CompilerParams(
            collective_id=0, has_side_effects=True, vmem_limit_bytes=58 * 2**20
        ),
        cost_estimate=pl.CostEstimate(
            flops=8_000_000_000, bytes_accessed=20_000_000, transcendentals=300_000
        ),
    )(
        tokens, out_grad, expert_ids.T, gate_values.T, wg[0], wu[0], wd[0],
        gf[0].T, gs[0], uf[0].T, us[0], df[0].T, ds[0],
    )
    tg, gg, ggi, ggo, gui, guo, gdi, gdo = pl.pallas_call(
        combine_kernel,
        out_shape=(
            shape((TD, D), bf16),
            shape((2, TD), f32),
            shape((16, D), f32),
            shape((16, F), f32),
            shape((16, D), f32),
            shape((16, F), f32),
            shape((16, F), f32),
            shape((16, D), f32),
        ),
        in_specs=[vmem] * 5,
        out_specs=[vmem] * 8,
        scratch_shapes=[pltpu.VMEM((NE, D), bf16)],
        compiler_params=pltpu.CompilerParams(vmem_limit_bytes=32 * 2**20),
    )(blocks, sel, permT, sums, expert_ids.T)
    return tg, gg.T, ggi.T[None], ggo[None], gui.T[None], guo[None], gdi.T[None], gdo[None]


def solution(mesh):
    row = P(("dp", "expert"), None)
    frozen = P("expert", "dp", None)
    one = P("expert", None, None)
    return jax.shard_map(
        per_device,
        mesh=mesh,
        in_specs=(row,) * 4 + (frozen,) * 3 + (one,) * 6,
        out_specs=(row,) * 2 + (one,) * 6,
        check_vma=False,
    )
```

```python
import functools

import jax
import jax.numpy as jnp
from jax import lax
from jax.experimental import pallas as pl
from jax.experimental.pallas import tpu as pltpu
from jax.sharding import PartitionSpec as P

MESH = pl.DeviceIdType.MESH
bf16 = jnp.bfloat16
f32 = jnp.float32
i32 = jnp.int32

NE, ND = 32, 16
TD, D, F = 128, 2560, 768
H = D // 2
SH = D // ND
ROWS = 288
BW = H + 256
PIECES = 9
SCALE = 2.0


def nn(a, b):
    return lax.dot_general(a, b, (((1,), (0,)), ((), ())), preferred_element_type=f32)


def nt(a, b):
    return lax.dot_general(a, b, (((1,), (1,)), ((), ())), preferred_element_type=f32)


def tn(a, b):
    return lax.dot_general(a, b, (((0,), (0,)), ((), ())), preferred_element_type=f32)


def iota(shape, axis):
    return lax.broadcasted_iota(i32, shape, axis)


def flag(mask):
    return jnp.where(mask, 1.0, 0.0).astype(bf16)


def loop(n, body):
    def step(k, carry):
        body(k)
        return carry

    lax.fori_loop(0, n, step, 0)


def lanes(n, width=256, start=0):
    return pl.ds(pl.multiple_of(n * width + start, 128), width)


def pair_slots(ids):
    e32 = iota((NE, TD), 0)
    id0, id1 = ids[0:1, :], ids[1:2, :]
    hot = [jnp.where(e32 == id0, 1.0, 0.0), jnp.where(e32 == id1, 1.0, 0.0)]
    earlier = flag(iota((TD, TD), 0) < iota((TD, TD), 1))
    before = nn((hot[0] + hot[1]).astype(bf16), earlier)
    slots = [jnp.sum(before * h, axis=0, keepdims=True).astype(i32) for h in hot]
    sel9 = (
        jnp.where(slots[0] == 8, hot[0], 0.0) + jnp.where(slots[1] == 8, hot[1], 0.0)
    ).astype(bf16)
    return id0, id1, hot, slots, sel9


def kernel(
    tok, grd, ids, gates, wg, wu, wd, in_gf, in_gs, in_uf, in_us, in_df, in_ds,
    block_out, sel_out, perm_out, ad_out,
    send, recv, wbuf, sel, perm, permT, fold, unfold, x, g, sg, coef, act, hid, ggp, ugp,
    ad_send, ad_recv, ad_one, ad_all, ad_far, ad_near,
    gfT, ufT, dsec, gs, us, dfT, staged, moved, packed, ad_moved, ad_buf,
    s_send, s_recv, st_sem, m_send, m_recv, x_send, x_recv, x_own,
    y1_send, y1_recv, y2_send, y2_recv, a_send, a_recv, f_send, f_recv, o_sem,
):
    me = lax.axis_index("expert")
    dp = lax.axis_index("dp")

    z, c = me // 2, me % 2
    y, xx = dp // 4, dp % 4
    b = dp % 2
    odd = (b + c) % 2

    mine = ((z + 16 + b * (14 * c - 7)) % 16) * 2 + c
    my_slot = b * 16 + (3 + odd) * 2 + c
    my_k = c + 2 * b + 4 * (3 + odd)
    z_to = (z + 23 - 14 * c) % 16
    z_from = (z + 9 + 14 * c) % 16

    def home(k):
        c2, b2, j = k % 2, (k // 2) % 2, k // 4
        zp = (z + 13 + j - (b2 + c2) % 2) % 16
        expert = ((zp + 16 + b2 * (14 * c2 - 7)) % 16) * 2 + c2
        return dp - b + b2, zp * 2 + c2, expert, b * 16 + j * 2 + c

    def origin(slot):
        cs, j, bs = slot % 2, (slot % 16) // 2, slot // 16
        zs = (z + 19 - j + odd) % 16
        return dp - b + bs, zs * 2 + cs

    def dp_peer(k):
        return (dp + 1 + k) % ND

    bar = pltpu.get_barrier_semaphore()

    def greet(d, e):
        pl.semaphore_signal(
            bar, inc=1, device_id={"dp": d, "expert": e}, device_id_type=MESH)

    def greet_rows(k):
        i = (2 * b + c + 16 + 1 + k) % 36
        greet(dp - b + (i // 2) % 2, ((z + 12 + i // 4) % 16) * 2 + i % 2)

    loop(35, greet_rows)
    greet(dp, z_to * 2 + c)
    greet(dp, z_from * 2 + c)
    loop(ND - 1, lambda k: greet(dp_peer(k), me))

    def block(p):
        return pl.ds(pl.multiple_of(p * 16, 16), 16)

    def row_copy(buf, src, dst, d, e):
        return pltpu.make_async_remote_copy(
            src_ref=send.at[buf, block(src)],
            dst_ref=recv.at[buf, block(dst)],
            send_sem=s_send.at[buf, src],
            recv_sem=s_recv.at[buf, dst],
            device_id={"dp": d, "expert": e},
            device_id_type=MESH,
        )

    def rows_start(buf):
        def body(i):
            d, e, expert, slot = home((my_k + 1 + i) % NE)
            row_copy(buf, expert, slot, d, e).start()

        loop(NE - 1, body)
        recv[buf, block(my_slot), :] = send[buf, block(mine), :]

    CUT = 768

    def back_copy(part, src, dst, d, e):
        c = pl.ds(0, CUT) if part == 0 else pl.ds(CUT, BW - CUT)
        return pltpu.make_async_remote_copy(
            src_ref=send.at[2, block(src), c],
            dst_ref=recv.at[2, block(dst), c],
            send_sem=s_send.at[2 + part, src],
            recv_sem=s_recv.at[2 + part, dst],
            device_id={"dp": d, "expert": e},
            device_id_type=MESH,
        )

    def rows_back(part):
        def body(i):
            slot = (my_slot + 1 + i) % NE
            d, e = origin(slot)
            back_copy(part, slot, mine, d, e).start()

        loop(NE - 1, body)
        c = slice(0, CUT) if part == 0 else slice(CUT, BW)
        recv[2, block(mine), c] = send[2, block(my_slot), c]

    def back_wait(part):
        loop(NE - 1, lambda i: back_copy(
            part, (mine + 1 + i) % NE, (mine + 1 + i) % NE, dp, z_to * 2 + c).wait_recv())

    def back_sent(part):
        loop(NE - 1, lambda i: back_copy(
            part, (my_slot + 1 + i) % NE, (my_slot + 1 + i) % NE, dp, z_to * 2 + c).wait_send())

    def rows_wait(buf, own):
        loop(NE - 1, lambda i: row_copy(
            buf, (own + 1 + i) % NE, (own + 1 + i) % NE, dp, z_to * 2 + c).wait_recv())

    def rows_sent(buf, own):
        loop(NE - 1, lambda i: row_copy(
            buf, (own + 1 + i) % NE, (own + 1 + i) % NE, dp, z_to * 2 + c).wait_send())

    AD = PIECES

    def stage(t):
        ref, n = ((wg, wu)[t % 2], t // 2) if t < 6 else (wd, t - 6)
        return pltpu.make_async_copy(
            ref.at[:, n * 256 : (n + 1) * 256], staged.at[t], st_sem.at[t])

    for t in range(PIECES):
        stage(t).start()

    def is_ad(t):
        return isinstance(t, int) and t == AD

    def first_of(t):
        return packed.at[dp] if is_ad(t) else staged.at[t]

    def second_of(t):
        return ad_moved if is_ad(t) else moved.at[t]

    def shard(t, d):
        if is_ad(t):
            return ad_buf.at[d]
        return wbuf.at[t, pl.ds(pl.multiple_of(d * SH, 32), SH)]

    def four(t, row, part):
        if is_ad(t):
            return ad_buf.at[pl.ds(row * 4 + (2 if part == 2 else 0), 2 if part else 4)]
        first = row * 4 * SH + (2 * SH if part == 2 else 0)
        return wbuf.at[t, pl.ds(pl.multiple_of(first, 64), (2 if part else 4) * SH)]

    def move(t):
        return pltpu.make_async_remote_copy(
            src_ref=first_of(t), dst_ref=second_of(t), send_sem=m_send.at[t], recv_sem=m_recv.at[t],
            device_id={"expert": z_to * 2 + c}, device_id_type=MESH,
        )

    def along_x(t, src, to, at):
        return pltpu.make_async_remote_copy(
            src_ref=src, dst_ref=shard(t, y * 4 + at),
            send_sem=x_send.at[t, to], recv_sem=x_recv.at[t, at],
            device_id={"dp": y * 4 + to}, device_id_type=MESH,
        )

    def x_start(t, stream):
        src = first_of(t) if stream == 0 else second_of(t)

        def body(i):
            to = stream + 2 * i

            @pl.when(to != xx)
            def _():
                along_x(t, src, to, xx).start()

            @pl.when(to == xx)
            def _():
                pltpu.make_async_copy(src, shard(t, dp), x_own.at[t]).start()

        loop(2, body)

    def x_wait(t):
        loop(3, lambda i: along_x(
            t, first_of(t), (xx + 1 + i) % 4, (xx + 1 + i) % 4).wait_recv())
        pltpu.make_async_copy(first_of(t), shard(t, dp), x_own.at[t]).wait()

    def x_sent(t):
        loop(3, lambda i: along_x(
            t, first_of(t), (xx + 1 + i) % 4, (xx + 1 + i) % 4).wait_send())

    ends = ((y + 1) % 4, (y + 3) % 4)

    def along_y(t, way, hop):
        region = four(t, y, 0) if hop == 1 else four(t, ends[1 - way], way + 1)
        sems = (y1_send, y1_recv) if hop == 1 else (y2_send, y2_recv)
        return pltpu.make_async_remote_copy(
            src_ref=region, dst_ref=region,
            send_sem=sems[0].at[t, way], recv_sem=sems[1].at[t, way],
            device_id={"dp": ends[way] * 4 + xx}, device_id_type=MESH,
        )

    def landed_y(t, way, hop):
        region = four(t, ends[1 - way], 0) if hop == 1 else four(t, (y + 2) % 4, way + 1)
        sems = (y1_send, y1_recv) if hop == 1 else (y2_send, y2_recv)
        pltpu.make_async_remote_copy(
            src_ref=region, dst_ref=region,
            send_sem=sems[0].at[t, way], recv_sem=sems[1].at[t, way],
            device_id={"dp": ends[way] * 4 + xx}, device_id_type=MESH,
        ).wait_recv()

    def move_done(t):
        move(t).wait_recv()
        x_start(t, 1)

    def y_first(t):
        x_wait(t)
        along_y(t, 0, 1).start()
        along_y(t, 1, 1).start()

    def y_second(t):
        for way in range(2):
            landed_y(t, way, 1)
            along_y(t, way, 2).start()

    def y_done(t):
        landed_y(t, 0, 2)
        landed_y(t, 1, 2)

    for first, ref in ((0, in_gf), (4, in_uf), (8, in_ds)):
        for j in range(4):
            packed[first + j] = ref[:, j * 640 : (j + 1) * 640]
    small = jnp.concatenate(
        [in_gs[...], in_us[...], in_df[...], jnp.zeros((16, 256), bf16)], axis=1
    )
    for j in range(4):
        packed[12 + j] = small[:, j * 640 : (j + 1) * 640]

    for t in range(PIECES):
        stage(t).wait()
    pl.semaphore_wait(bar, 35 + 2 + ND - 1)
    move(AD).start()
    loop(PIECES, lambda t: move(t).start())
    x_start(AD, 0)
    loop(PIECES, lambda t: x_start(t, 0))

    id0, id1, hot, slots, sel9 = pair_slots(ids)
    q512 = iota((512, TD), 0)
    keys = [
        jnp.where(slots[0] < 8, id0 * 16 + slots[0], -16),
        jnp.where(slots[1] < 8, id1 * 16 + slots[1], -16),
    ]
    sel[:, 0:TD] = flag((q512 == keys[0]) | (q512 == keys[1]))
    sel[:, TD : 2 * TD] = flag((q512 == keys[0] + 8) | (q512 == keys[1] + 8))
    qa, qb = iota((512, 512), 0), iota((512, 512), 1)
    perm[...] = flag(qb == (qa % 16) * 32 + qa // 16)
    permT[...] = flag(qa == (qb % 16) * 32 + qb // 16)
    cb = qb % 256
    fold[...] = flag(qa == (cb // 8) * 16 + cb % 8 + (qb // 256) * 8)
    ca = qa % 256
    unfold[...] = flag(qb == (ca // 8) * 16 + ca % 8 + (qa // 256) * 8)
    put_weight = flag(iota((512, NE), 0) == iota((512, NE), 1) * 16 + 4)
    take_weight = flag(iota((NE, 512), 1) == iota((NE, 512), 0) * 16 + 4)


    def tail_to_block(buf, nine, extra):
        first = jnp.concatenate([nine[:, j * 128 : (j + 1) * 128] for j in range(16)], axis=0)
        last = jnp.concatenate([nine[:, j * 128 : (j + 1) * 128] for j in range(16, 20)], axis=0)
        send[buf, :, H : H + 128] = nn(perm[...], first).astype(bf16)
        z1 = nn(perm[:, 0:128], last)
        if extra is not None:
            z1 = z1 + nn(put_weight, extra)
        send[buf, :, H + 128 : BW] = z1.astype(bf16)

    def tail_from_block(buf):
        first = nn(permT[...], recv[buf, :, H : H + 128]).astype(bf16)
        last = nn(permT[0:128, :], recv[buf, :, H + 128 : BW]).astype(bf16)
        parts = [first[j * 32 : (j + 1) * 32] for j in range(16)]
        parts += [last[j * 32 : (j + 1) * 32] for j in range(4)]
        return parts

    def dispatch(buf, src, extra):
        def body(n):
            both = jnp.concatenate([src[:, lanes(n)], src[:, lanes(n, start=H)]], axis=0)
            send[buf, :, lanes(n)] = nn(sel[...], both).astype(bf16)

        loop(H // 256, body)
        tail_to_block(buf, nn(sel9, src[...]).astype(bf16), extra)

    dispatch(0, tok, None)
    rows_start(0)
    sel_copy = pltpu.make_async_copy(sel, sel_out, o_sem.at[0])
    sel_copy.start()
    perm_copy = pltpu.make_async_copy(permT, perm_out, o_sem.at[1])
    perm_copy.start()
    r128 = iota((128, TD), 0)
    weights = 0.0
    for k in range(2):
        a = (hot[k] * gates[k : k + 1, :]).astype(bf16)
        weights = weights + nt(a, flag(r128 == slots[k]))
    dispatch(1, grd, weights.astype(bf16))
    rows_start(1)

    move_done(AD)
    move_done(0)
    y_first(AD)
    move_done(1)
    y_first(0)
    y_second(AD)

    def relay(i):
        move_done(i + 2)
        y_first(i + 1)
        y_second(i)

    loop(PIECES - 2, relay)
    y_first(PIECES - 1)

    def receive(buf, dst):
        def body(n):
            both = nn(unfold[...], recv[buf, :, lanes(n)]).astype(bf16)
            dst[0:256, lanes(n)] = both[0:256]
            dst[0:256, lanes(n, start=H)] = both[256:512]

        loop(H // 256, body)
        for j, part in enumerate(tail_from_block(buf)):
            dst[256:ROWS, j * 128 : (j + 1) * 128] = part

    rows_wait(0, my_slot)
    receive(0, x)
    y_done(AD)

    def load4(buf, first):
        return jnp.concatenate([buf[first + j] for j in range(4)], axis=1)

    gfT[...] = load4(ad_buf, 0)
    ufT[...] = load4(ad_buf, 4)
    dsec[...] = load4(ad_buf, 8)
    rest = load4(ad_buf, 12)
    gs[...] = rest[:, 0:F]
    us[...] = rest[:, F : 2 * F]
    dfT[...] = rest[:, 2 * F : 3 * F]
    low = nt(x[...], jnp.concatenate([gfT[...], ufT[...]], axis=0)).astype(bf16)
    gate_low, up_low = low[:, 0:16], low[:, 16:32]
    y_second(PIECES - 2)
    y_second(PIECES - 1)

    def forward(n):
        c = lanes(n)
        y_done(2 * n)
        pre = nn(x[...], wbuf[2 * n]) + SCALE * nn(gate_low, gs[:, c])
        y_done(2 * n + 1)
        up = nn(x[...], wbuf[2 * n + 1]) + SCALE * nn(up_low, us[:, c])
        s = jax.nn.sigmoid(pre)
        a = pre * s
        act[:, c] = a
        coef[:, c] = up * s * (1.0 + pre * (1.0 - s))
        hid[:, c] = (a * up).astype(bf16)

    loop(F // 256, forward)
    hidden_low = nt(hid[...], dfT[...]).astype(bf16)

    rows_wait(1, my_slot)
    receive(1, g)
    wt = nn(take_weight, recv[1, :, H + 128 : BW])
    p256 = iota((256, 128), 0)
    l256 = iota((256, 128), 1)
    spread = flag(iota((256, NE), 0) // 8 == iota((256, NE), 1))
    gather = flag(iota((NE, 256), 1) // 8 == iota((NE, 256), 0))
    diag = l256 == p256 % 8
    ninth = iota((NE, 128), 1) == 8
    w_main = jnp.sum(jnp.where(diag, nn(spread, wt.astype(bf16)), 0.0), axis=1, keepdims=True)
    w_nine = jnp.sum(jnp.where(ninth, wt, 0.0), axis=1, keepdims=True)
    weight = jnp.concatenate([w_main, w_nine], axis=0)
    u_low = nt(g[...], dsec[...])
    cot_low = (weight * u_low).astype(bf16)
    sg0 = SCALE * jnp.sum(hidden_low.astype(f32) * u_low, axis=1, keepdims=True)
    bgl = jnp.zeros((ROWS, 16), f32)
    bul = jnp.zeros((ROWS, 16), f32)

    def backward(n, carry):
        slot_gate, bg, bu = carry
        c = lanes(n)
        y_done(6 + n)
        u = nn(g[...], wbuf[6 + n])
        slot_gate = slot_gate + jnp.sum(hid[:, c].astype(f32) * u, axis=1, keepdims=True)
        hg = weight * u + SCALE * nn(cot_low, dfT[:, c])
        gg = (hg * coef[:, c]).astype(bf16)
        ug = (hg * act[:, c]).astype(bf16)
        ggp[:, c] = gg
        ugp[:, c] = ug
        return slot_gate, bg + nt(gg, gs[:, c]), bu + nt(ug, us[:, c])

    slot_gate, bgl, bul = lax.fori_loop(0, F // 256, backward, (sg0, bgl, bul))
    bgl = bgl.astype(bf16)
    bul = bul.astype(bf16)

    def slot_grad(n):
        c = pl.ds(pl.multiple_of(n * 256, 256), 256)
        value = SCALE * (nn(bgl, gfT[:, c]) + nn(bul, ufT[:, c]))
        for k in range(3):
            f = slice(k * 256, (k + 1) * 256)
            value = value + nt(ggp[:, f], wbuf[2 * k, c, :])
            value = value + nt(ugp[:, f], wbuf[2 * k + 1, c, :])
        sg[:, c] = value.astype(bf16)

    def pack(n):
        both = jnp.concatenate([sg[0:256, lanes(n)], sg[0:256, lanes(n, start=H)]], axis=0)
        send[2, :, lanes(n)] = nn(fold[...], both).astype(bf16)

    def both_halves(n):
        slot_grad(n)
        slot_grad(n + H // 256)
        pack(n)

    loop(CUT // 256, both_halves)
    rows_back(0)

    bl = jnp.concatenate([bgl, bul], axis=1)

    def store4(first, value):
        for j in range(4):
            ad_send[first + j] = value[:, j * 640 : (j + 1) * 640]

    ins = (SCALE * tn(bl, x[...])).astype(bf16)
    store4(0, ins[0:16])
    store4(4, ins[16:32])
    whl = (weight * hidden_low.astype(f32)).astype(bf16)
    store4(8, (SCALE * tn(whl, g[...])).astype(bf16))
    store4(12, jnp.concatenate([
        (SCALE * tn(gate_low, ggp[...])).astype(bf16),
        (SCALE * tn(up_low, ugp[...])).astype(bf16),
        (SCALE * tn(cot_low, hid[...])).astype(bf16),
        jnp.zeros((16, 256), bf16),
    ], axis=1))

    def part_copy(phase, there, here):
        if phase == 0:
            src, dst = ad_send.at[there], ad_recv.at[here]
        else:
            src, dst = ad_one, ad_all.at[here]
        return pltpu.make_async_remote_copy(
            src_ref=src,
            dst_ref=dst,
            send_sem=a_send.at[phase, there],
            recv_sem=a_recv.at[phase, here],
            device_id={"dp": there},
            device_id_type=MESH,
        )

    def part_wait(phase):
        def body(k):
            p = dp_peer(k)
            part_copy(phase, p, p).wait()

        loop(ND - 1, body)

    loop(ND - 1, lambda k: part_copy(0, dp_peer(k), dp).start())
    ad_recv[dp] = ad_send[dp]

    loop(H // 256 - CUT // 256, lambda n: both_halves(n + CUT // 256))
    back = nn(gather, jnp.where(diag, slot_gate[0:256], 0.0).astype(bf16))
    back = back + jnp.where(ninth, slot_gate[256:ROWS], 0.0)
    tail_to_block(2, sg[256:ROWS, :], back.astype(bf16))
    part_wait(0)

    def both(j, t):
        return t[0] + ad_recv[2 * j].astype(f32), t[1] + ad_recv[2 * j + 1].astype(f32)

    zero = jnp.zeros((16, 640), f32)
    here, there = lax.fori_loop(0, ND // 2, both, (zero, zero))
    ad_far[...] = there
    far = pltpu.make_async_remote_copy(
        src_ref=ad_far, dst_ref=ad_near, send_sem=f_send.at[0], recv_sem=f_recv.at[0],
        device_id={"expert": z_from * 2 + c}, device_id_type=MESH,
    )
    far.start()
    rows_back(1)

    far.wait()
    total = (here + ad_near[...]).astype(bf16)
    ad_one[...] = total
    loop(ND - 1, lambda k: part_copy(1, dp_peer(k), dp).start())
    ad_all[dp] = total
    part_wait(1)

    ad_copy = pltpu.make_async_copy(ad_all, ad_out, o_sem.at[2])
    ad_copy.start()

    def all_sent(t):
        move(t).wait_send()
        x_sent(t)
        for way in range(2):
            along_y(t, way, 1).wait_send()
            along_y(t, way, 2).wait_send()

    all_sent(AD)
    loop(PIECES, all_sent)
    rows_sent(0, mine)
    rows_sent(1, mine)
    back_sent(0)
    back_sent(1)
    back_wait(0)
    back_wait(1)
    block_copy = pltpu.make_async_copy(recv.at[2], block_out, o_sem.at[3])
    block_copy.start()
    for copy in (sel_copy, perm_copy, ad_copy, block_copy):
        copy.wait()


def combine_kernel(
    blocks, sel, permT, sums, ids, tg_out, gg_out, ggi, ggo, gui, guo, gdi, gdo, sg
):
    _, _, hot, slots, sel9 = pair_slots(ids)
    first = nn(permT[...], blocks[:, H : H + 128]).astype(bf16)
    last = nn(permT[0:128, :], blocks[:, H + 128 : BW]).astype(bf16)
    for j in range(16):
        sg[:, j * 128 : (j + 1) * 128] = first[j * 32 : (j + 1) * 32]
    for j in range(4):
        sg[:, (16 + j) * 128 : (17 + j) * 128] = last[j * 32 : (j + 1) * 32]

    def combine(n):
        r = blocks[:, lanes(n)]
        left = tn(sel[:, 0:TD], r) + tn(sel9, sg[:, lanes(n)])
        right = tn(sel[:, TD : 2 * TD], r) + tn(sel9, sg[:, lanes(n, start=H)])
        tg_out[:, lanes(n)] = left.astype(bf16)
        tg_out[:, lanes(n, start=H)] = right.astype(bf16)

    loop(H // 256, combine)
    take_weight = flag(iota((NE, 512), 1) == iota((NE, 512), 0) * 16 + 4)
    r128 = iota((128, TD), 0)
    wt3 = nn(take_weight, blocks[:, H + 128 : BW]).astype(bf16)
    for k in range(2):
        picked = tn(wt3, hot[k].astype(bf16))
        gg_out[k : k + 1, :] = jnp.sum(
            jnp.where(r128 == slots[k], picked, 0.0), axis=0, keepdims=True
        )

    def load4(first):
        return jnp.concatenate([sums[first + j] for j in range(4)], axis=1).astype(f32)

    ggi[...] = load4(0)
    gui[...] = load4(4)
    gdo[...] = load4(8)
    rest = load4(12)
    ggo[...] = rest[:, 0:F]
    guo[...] = rest[:, F : 2 * F]
    gdi[...] = rest[:, 2 * F : 3 * F]


def per_device(tokens, out_grad, expert_ids, gate_values, wg, wu, wd, gf, gs, uf, us, df, ds):
    vmem = pl.BlockSpec(memory_space=pltpu.VMEM)
    anywhere = pl.BlockSpec(memory_space=pl.ANY)
    shape = jax.ShapeDtypeStruct
    blocks, sel, permT, sums = pl.pallas_call(
        kernel,
        out_shape=(
            shape((512, BW), bf16),
            shape((512, 2 * TD), bf16),
            shape((512, 512), bf16),
            shape((16, 16, 640), bf16),
        ),
        in_specs=[vmem] * 4 + [anywhere] * 3 + [vmem] * 6,
        out_specs=[anywhere] * 4,
        scratch_shapes=[
            pltpu.VMEM((3, 512, BW), bf16),
            pltpu.VMEM((3, 512, BW), bf16),
            pltpu.VMEM((PIECES, D, 256), bf16),
            pltpu.VMEM((512, 2 * TD), bf16),
            pltpu.VMEM((512, 512), bf16),
            pltpu.VMEM((512, 512), bf16),
            pltpu.VMEM((512, 512), bf16),
            pltpu.VMEM((512, 512), bf16),
            pltpu.VMEM((ROWS, D), bf16),
            pltpu.VMEM((ROWS, D), bf16),
            pltpu.VMEM((ROWS, D), bf16),
            pltpu.VMEM((ROWS, F), f32),
            pltpu.VMEM((ROWS, F), f32),
            pltpu.VMEM((ROWS, F), bf16),
            pltpu.VMEM((ROWS, F), bf16),
            pltpu.VMEM((ROWS, F), bf16),
            pltpu.VMEM((16, 16, 640), bf16),
            pltpu.VMEM((16, 16, 640), bf16),
            pltpu.VMEM((16, 640), bf16),
            pltpu.VMEM((16, 16, 640), bf16),
            pltpu.VMEM((16, 640), f32),
            pltpu.VMEM((16, 640), f32),
            pltpu.VMEM((16, D), bf16),
            pltpu.VMEM((16, D), bf16),
            pltpu.VMEM((16, D), bf16),
            pltpu.VMEM((16, F), bf16),
            pltpu.VMEM((16, F), bf16),
            pltpu.VMEM((16, F), bf16),
            pltpu.VMEM((PIECES, SH, 256), bf16),
            pltpu.VMEM((PIECES, SH, 256), bf16),
            pltpu.VMEM((16, 16, 640), bf16),
            pltpu.VMEM((16, 640), bf16),
            pltpu.VMEM((16, 16, 640), bf16),
            pltpu.SemaphoreType.DMA((4, NE)),
            pltpu.SemaphoreType.DMA((4, NE)),
            pltpu.SemaphoreType.DMA((PIECES,)),
            pltpu.SemaphoreType.DMA((PIECES + 1,)),
            pltpu.SemaphoreType.DMA((PIECES + 1,)),
            pltpu.SemaphoreType.DMA((PIECES + 1, 4)),
            pltpu.SemaphoreType.DMA((PIECES + 1, 4)),
            pltpu.SemaphoreType.DMA((PIECES + 1,)),
            pltpu.SemaphoreType.DMA((PIECES + 1, 2)),
            pltpu.SemaphoreType.DMA((PIECES + 1, 2)),
            pltpu.SemaphoreType.DMA((PIECES + 1, 2)),
            pltpu.SemaphoreType.DMA((PIECES + 1, 2)),
            pltpu.SemaphoreType.DMA((2, ND)),
            pltpu.SemaphoreType.DMA((2, ND)),
            pltpu.SemaphoreType.DMA((1,)),
            pltpu.SemaphoreType.DMA((1,)),
            pltpu.SemaphoreType.DMA((4,)),
        ],
        compiler_params=pltpu.CompilerParams(
            collective_id=0, has_side_effects=True, vmem_limit_bytes=58 * 2**20
        ),
        cost_estimate=pl.CostEstimate(
            flops=8_000_000_000, bytes_accessed=20_000_000, transcendentals=300_000
        ),
    )(
        tokens, out_grad, expert_ids.T, gate_values.T, wg[0], wu[0], wd[0],
        gf[0].T, gs[0], uf[0].T, us[0], df[0].T, ds[0],
    )
    tg, gg, ggi, ggo, gui, guo, gdi, gdo = pl.pallas_call(
        combine_kernel,
        out_shape=(
            shape((TD, D), bf16),
            shape((2, TD), f32),
            shape((16, D), f32),
            shape((16, F), f32),
            shape((16, D), f32),
            shape((16, F), f32),
            shape((16, F), f32),
            shape((16, D), f32),
        ),
        in_specs=[vmem] * 5,
        out_specs=[vmem] * 8,
        scratch_shapes=[pltpu.VMEM((NE, D), bf16)],
        compiler_params=pltpu.CompilerParams(vmem_limit_bytes=32 * 2**20),
    )(blocks, sel, permT, sums, expert_ids.T)
    return tg, gg.T, ggi.T[None], ggo[None], gui.T[None], guo[None], gdi.T[None], gdo[None]


def solution(mesh):
    row = P(("dp", "expert"), None)
    frozen = P("expert", "dp", None)
    one = P("expert", None, None)
    return jax.shard_map(
        per_device,
        mesh=mesh,
        in_specs=(row,) * 4 + (frozen,) * 3 + (one,) * 6,
        out_specs=(row,) * 2 + (one,) * 6,
        check_vma=False,
    )
```
